512 devices in a mesh: depth: 32 (over z_hi, x, core), plan: 16 (over y, z_lo).
Axes of the slice: x: 4, y: 8, z: 8 (z_hi: 4, z_lo: 2; z = z_hi * 2 + z_lo), core: 2. Of those that a mesh axis runs over, the one named last changes fastest.
Arguments:
- stress: float32 [6, 256, 256, 256], P(None, 'depth', 'plan'), may hold values from -6 to 6
- velocity: float32 [3, 256, 256, 256], P(None, 'depth', 'plan'), may hold values from -3 to 3
- density: float32 [256, 256, 256], P('depth', 'plan'), may hold values from 1 to 4
- branch_flags: int32 [256, 256, 256], P('depth', 'plan'), may hold values from 0 to 2
- pile_velocity: float32 [3, 196608], P(None, 'depth'), may hold values from -3 to 3
- pile_mass: float32 [196608], P('depth'), may hold values from 0.5 to 2
- jack_force: float32 [3, 196608], P(None, 'depth'), may hold values from -6 to 6
- pair_elem: int32 [32, 32768], P('depth', 'plan'), may hold values from 0 to 18431, as said below
- pair_cell: int32 [32, 32768], P('depth', 'plan'), may hold values from -1 to 32767, as said below
Outputs:
- stress_out: float32 [6, 256, 256, 256], P(None, 'depth', 'plan')
- velocity_out: float32 [3, 256, 256, 256], P(None, 'depth', 'plan')
- pile_velocity_out: float32 [3, 196608], P(None, 'depth')
The draws below stay inside these ranges and needn't reach their ends.
Inputs may be any that keep to these rules, and one draw needn't show every extreme that they name: `pair_elem`: counted from block d - 1 for depth index d, it names an element of the pile: blocks d - 1, d, d + 1 only, never below block 0 or above the last block. `pair_cell`: live pairs (cell >= 0) of one device are its first slots; at most 2048 on one device; all slots live on every device of one depth index, the tip, which lies above the middle depth index and below the last; fewer live on the depth indices before it, none after it.
All inputs are finite; a program needn't handle non-finite values.
Results may differ from the reference program's by a relative error of at most 0.00016.
Values sent between devices are 32-bit elements; how exact they have to be, the bound alone decides.
A program may use at most 64 MiB of HBM per device.

```python
import math
import jax
import jax.numpy as jnp

CZ = 8
CX = 16
CY = 256
PILE_DEV = 6144
PAIRS_DEV = 2048
STEPS = 3
NZ = 256
NX = 256
PILE = 196608
N_DEPTH = 32
N_PLAN = 16


def tip_layout(key):
    tip_slab = jax.random.randint(jax.random.fold_in(key, 11), (), N_DEPTH // 2 + 1, N_DEPTH - 1)
    row_ids = jnp.arange(N_DEPTH, dtype=jnp.int32)[:, None]
    col_ids = jnp.arange(N_PLAN * PAIRS_DEV, dtype=jnp.int32)[None, :]
    slot_ids = col_ids % PAIRS_DEV
    live_count = jnp.where(row_ids == tip_slab, PAIRS_DEV, jnp.where(row_ids < tip_slab, PAIRS_DEV // 3, 0))
    return (row_ids, slot_ids < live_count)


def draw_pair_elem(key, part):
    row_ids, is_live = tip_layout(key)
    lowest = jnp.where(row_ids == 0, PILE_DEV, 0)
    highest = jnp.where(row_ids == N_DEPTH - 1, 2 * PILE_DEV, 3 * PILE_DEV)
    drawn = jax.random.randint(jax.random.fold_in(key, 12), (N_DEPTH, N_PLAN * PAIRS_DEV), 0, 3 * PILE_DEV)
    return (lowest + drawn % (highest - lowest)).astype(jnp.int32)


def draw_pair_cell(key, part):
    row_ids, is_live = tip_layout(key)
    drawn = jax.random.randint(jax.random.fold_in(key, 13), (N_DEPTH, N_PLAN * PAIRS_DEV), 0, CZ * CX * CY)
    return jnp.where(is_live, drawn, -1).astype(jnp.int32)


def touch_ends(array, own_key, least, high):
    longest = array.shape.index(max(array.shape))
    spots = []
    for shift in (0, 1):
        where = [jax.random.randint(jax.random.fold_in(own_key, axis), (), 0, length) for axis, length in enumerate(array.shape)]
        where[longest] = (where[longest] + shift) % array.shape[longest]
        spots.append(tuple(where))
    return array.at[spots[0]].set(least).at[spots[1]].set(high)


def shard_levels(own_key, extent, shards, smallest, high):
    def one(position, blocks):
        heights = jax.random.uniform(jax.random.fold_in(jax.random.fold_in(own_key, 6), position), (blocks,), jnp.float32, smallest / len(shards), high / len(shards))
        return jnp.repeat(jnp.exp(heights), extent[position] // blocks).reshape((-1,) + (1,) * (len(extent) - position - 1))

    factor_of = one(*shards[0])
    for cut in shards[1:]:
        factor_of = factor_of * one(*cut)
    return factor_of


def scatter_about(rng, dims, scale, most, split=(), held_as=jnp.bfloat16):
    result = jax.random.normal(rng, dims, jnp.float32) * scale
    if len(split) > 0:
        result = shard_levels(rng, dims, split, -0.22, 0.18) * result
    return jnp.clip(result, min=-most, max=most).astype(held_as)


def setup_inputs(seed: int = 0) -> dict:
    arg_keys = jax.random.split(jax.random.key(seed), 10)
    return {
        "stress": scatter_about(arg_keys[0], (6, NZ, NX, CY), 1.0, 6.0, ((1, 32), (2, 16)), jnp.float32),
        "velocity": scatter_about(arg_keys[1], (3, NZ, NX, CY), 0.5, 3.0, ((1, 32), (2, 16)), jnp.float32),
        "density": jnp.clip(jnp.exp(math.log(4.0) - 1.3862944 * jax.random.uniform(arg_keys[2], (NZ, NX, CY), jnp.float32) ** shard_levels(arg_keys[2], (NZ, NX, CY), ((0, 32), (1, 16)), -0.2, 0.2)), 1.0, 4.0),
        "branch_flags": touch_ends(jax.random.randint(arg_keys[3], (NZ, NX, CY), 0, 3), jax.random.fold_in(arg_keys[3], 1), 0, 2).astype(jnp.int32),
        "pile_velocity": scatter_about(arg_keys[4], (3, PILE), 0.5, 3.0, ((1, 32),), jnp.float32),
        "pile_mass": jnp.clip(jnp.exp(math.log(2.0) - 1.3862944 * jax.random.uniform(arg_keys[5], (PILE,), jnp.float32) ** shard_levels(arg_keys[5], (PILE,), ((0, 32),), -0.2, 0.2)), 0.5, 2.0),
        "jack_force": scatter_about(arg_keys[6], (3, PILE), 1.0, 6.0, ((1, 32),), jnp.float32),
        "pair_elem": draw_pair_elem(jax.random.fold_in(arg_keys[9], 71), 0),
        "pair_cell": draw_pair_cell(jax.random.fold_in(arg_keys[9], 71), 0),
    }


time_step = 0.2
penalty = 1.0
lame_first = 1.0
shear_modulus = 1.0
cone_rate = 1.5
symmetric_index = ((0, 3, 4), (3, 1, 5), (4, 5, 2))

def slopes_of(padded):
    along_depth = 0.5 * (padded[:, 2:, 1:-1, 1:-1] - padded[:, :-2, 1:-1, 1:-1])
    along_plan = 0.5 * (padded[:, 1:-1, 2:, 1:-1] - padded[:, 1:-1, :-2, 1:-1])
    along_last = 0.5 * (padded[:, 1:-1, 1:-1, 2:] - padded[:, 1:-1, 1:-1, :-2])
    return (along_depth, along_plan, along_last)

def divergence(padded):
    slopes = slopes_of(padded)
    return jnp.stack([slopes[0][symmetric_index[component][0]] + slopes[1][symmetric_index[component][1]] + slopes[2][symmetric_index[component][2]] for component in range(3)])

def strain_rate(padded):
    slopes = slopes_of(padded)
    return jnp.stack([slopes[0][0], slopes[1][1], slopes[2][2], 0.5 * (slopes[1][0] + slopes[0][1]), 0.5 * (slopes[2][0] + slopes[0][2]), 0.5 * (slopes[2][1] + slopes[1][2])])

def return_map(trial_stress, branch_flags):
    pressure = (trial_stress[0] + trial_stress[1] + trial_stress[2]) / 3.0
    deviator = jnp.stack([trial_stress[0] - pressure, trial_stress[1] - pressure, trial_stress[2] - pressure, trial_stress[3], trial_stress[4], trial_stress[5]])
    second = 0.5 * (deviator[0] * deviator[0] + deviator[1] * deviator[1] + deviator[2] * deviator[2]) + deviator[3] * deviator[3] + deviator[4] * deviator[4] + deviator[5] * deviator[5]
    shrink = 1.0 / (1.0 + cone_rate * jnp.sqrt(second))
    empty_part = jnp.zeros_like(pressure)
    spherical = jnp.stack([pressure, pressure, pressure, empty_part, empty_part, empty_part])
    cone_stress = deviator * shrink + spherical
    return jnp.where(branch_flags == 0, trial_stress, jnp.where(branch_flags == 1, cone_stress, spherical))

def stress_update(stress, padded_velocity, branch_flags):
    strain = strain_rate(padded_velocity)
    increment = 2.0 * shear_modulus * strain
    increment = increment.at[:3].add(lame_first * (strain[0] + strain[1] + strain[2]))
    return return_map(stress + time_step * increment, branch_flags)

def pad_cells(field):
    return jnp.pad(field, ((0, 0), (1, 1), (1, 1), (1, 1)))

def reference(stress, velocity, density, branch_flags, pile_velocity, pile_mass, jack_force, pair_elem, pair_cell):
    row_ids = jnp.arange(N_DEPTH, dtype=jnp.int32)[:, None]
    col_ids = jnp.arange(N_PLAN * PAIRS_DEV, dtype=jnp.int32)[None, :]
    plan_ids = col_ids // PAIRS_DEV
    weight = (pair_cell >= 0).astype(jnp.float32).reshape(-1)
    clamped = jnp.maximum(pair_cell, 0)
    depth_cell = row_ids * CZ + clamped // (CX * CY)
    plan_cell = plan_ids * CX + clamped // CY % CX
    last_cell = clamped % CY
    cell_index = ((depth_cell * NX + plan_cell) * CY + last_cell).reshape(-1).astype(jnp.int32)
    elem_index = jnp.clip((row_ids - 1) * PILE_DEV + pair_elem, 0, PILE - 1).reshape(-1).astype(jnp.int32)
    for step_number in range(STEPS):
        stress_force = divergence(pad_cells(stress))
        flat_velocity = velocity.reshape(3, -1)
        pushes = penalty * (pile_velocity[:, elem_index] - flat_velocity[:, cell_index]) * weight
        on_cells = jnp.zeros_like(flat_velocity).at[:, cell_index].add(pushes).reshape(velocity.shape)
        on_pile = jnp.zeros_like(pile_velocity).at[:, elem_index].add(pushes)
        velocity = velocity + time_step * (stress_force + on_cells) / density
        pile_velocity = pile_velocity + time_step * (jack_force - on_pile) / pile_mass
        stress = stress_update(stress, pad_cells(velocity), branch_flags)
    return (stress, velocity, pile_velocity)
```

```python
import functools

import jax
import jax.numpy as jnp
from jax import lax
from jax.experimental import pallas as pl
from jax.experimental.pallas import tpu as pltpu
from jax.sharding import PartitionSpec as P

STEPS = 3
DT = 0.2
MESH = pl.DeviceIdType.MESH
F32 = jnp.float32
BF16 = jnp.bfloat16
SYM = ((0, 3, 4), (3, 1, 5), (4, 5, 2))
HALF_ROWS = 8


def split_two(x):
    high = x.astype(BF16)
    return high, (x - high.astype(F32)).astype(BF16)


def dot_nn(a, b):
    return jnp.dot(a, b, preferred_element_type=F32)


def dot_nt(a, b):
    return lax.dot_general(a, b, (((1,), (1,)), ((), ())), preferred_element_type=F32)


def along_y(a, lane, width):
    after = jnp.where(lane < width - 1, pltpu.roll(a, width - 1, 1), 0.0)
    before = jnp.where(lane > 0, pltpu.roll(a, 1, 1), 0.0)
    return after - before


def updated_stress(sig, dz, dx, dy, elastic, cone):
    half = 0.5 * DT
    common = half * (dz[0] + dx[1] + dy[2])
    trial = [
        sig[0] + DT * dz[0] + common,
        sig[1] + DT * dx[1] + common,
        sig[2] + DT * dy[2] + common,
        sig[3] + half * (dx[0] + dz[1]),
        sig[4] + half * (dy[0] + dz[2]),
        sig[5] + half * (dy[1] + dx[2]),
    ]
    pressure = (trial[0] + trial[1] + trial[2]) * (1.0 / 3.0)
    dev = [trial[i] - pressure for i in range(3)]
    second = 0.5 * (dev[0] * dev[0] + dev[1] * dev[1] + dev[2] * dev[2]) + (
        trial[3] * trial[3] + trial[4] * trial[4] + trial[5] * trial[5]
    )
    shrink = 1.0 / (1.0 + 1.5 * jnp.sqrt(second))
    factor = jnp.where(elastic, 1.0, jnp.where(cone, shrink, 0.0))
    new = [dev[i] * factor + pressure for i in range(3)]
    return new + [trial[i] * factor for i in range(3, 6)]


def kernel(
    sizes,
    stress,
    velocity,
    density,
    flags,
    pile0,
    mass,
    jack,
    pair_elem,
    pair_cell,
    stress_out,
    velocity_out,
    pile_out,
    sig,
    vx,
    v0,
    scale,
    flg,
    sigp,
    spk,
    pbuf,
    rxp,
    cbuf,
    crx,
    pvw,
    massv,
    jackv,
    elemv,
    cellv,
    crow,
    prow,
    acol,
    arow,
    bcol,
    brow,
    thi,
    tlo,
    phi,
    plo,
    acc_s,
    acc_c,
    count_c,
    sbuf,
    sdep,
    sown,
    rx,
    rxn,
    nown,
    local_sem,
    init_send,
    init_recv,
    halo_send,
    halo_recv,
    dep_send,
    dep_recv,
    part_send,
    part_recv,
    num_send,
    num_recv,
    all_send,
    all_recv,
    win_send,
    win_recv,
):
    depth_count, plan_count, cz, cx, cy, tiles, pairs, chunk = sizes
    units = 3 * tiles
    slots = -(-units // plan_count)
    rows = cz * cx
    prows = brow.shape[0]
    block_rows = tiles // 2 * 8
    d = lax.axis_index("depth")
    p = lax.axis_index("plan")
    d_up = lax.rem(d + 1, depth_count)
    d_dn = lax.rem(d + depth_count - 1, depth_count)
    p_up = lax.rem(p + 1, plan_count)
    p_dn = lax.rem(p + plan_count - 1, plan_count)
    own = pl.ds(8, cx)

    def remote(src, dst, send, recv, dd, pp):
        return pltpu.make_async_remote_copy(
            src_ref=src,
            dst_ref=dst,
            send_sem=send,
            recv_sem=recv,
            device_id={"depth": dd, "plan": pp},
            device_id_type=MESH,
        )

    local = [
        (stress, sig.at[:, pl.ds(1, cz), own, :]),
        (velocity, v0),
        (density, scale),
        (flags, flg.at[pl.ds(1, cz)]),
        (pile0, pvw.at[0, 1]),
        (mass, massv),
        (jack, jackv),
        (pair_elem, elemv),
        (pair_cell, cellv),
    ]
    local = [
        pltpu.make_async_copy(src, dst, local_sem.at[i]) for i, (src, dst) in enumerate(local)
    ]
    for copy in local:
        copy.start()

    barrier = pltpu.get_barrier_semaphore()
    corners = ((d_dn, p_dn), (d_dn, p_up), (d_up, p_dn), (d_up, p_up))
    for dd, pp in ((d_dn, p), (d_up, p)) + corners:
        pl.semaphore_signal(
            barrier, inc=1, device_id={"depth": dd, "plan": pp}, device_id_type=MESH
        )

    def greet(k, unused):
        pl.semaphore_signal(
            barrier,
            inc=1,
            device_id={"depth": d, "plan": lax.rem(p + k, plan_count)},
            device_id_type=MESH,
        )
        return unused

    lax.fori_loop(1, plan_count, greet, 0)
    for i in (0, 3):
        local[i].wait()

    def pack_edges(z, unused):
        at = pl.ds(z, 1)
        for c in range(6):
            spk[0, c, at, :] = sig[c, z + 1, 8:9, :]
            spk[1, c, at, :] = sig[c, z + 1, cx + 7 : cx + 8, :]
        spk[0, 6, at, :] = flg[z + 1, 0:1, :].astype(F32)
        spk[1, 6, at, :] = flg[z + 1, cx - 1 : cx, :].astype(F32)
        return unused

    lax.fori_loop(0, cz, pack_edges, 0)
    pl.semaphore_wait(barrier, plan_count + 5)

    init = [
        remote(pile0, pvw.at[0, 0], init_send.at[0], init_recv.at[0], d_up, p),
        remote(pile0, pvw.at[0, 2], init_send.at[1], init_recv.at[1], d_dn, p),
        remote(
            stress.at[:, cz - 1], sig.at[:, 0, own, :], init_send.at[2], init_recv.at[2], d_up, p
        ),
        remote(
            stress.at[:, 0], sig.at[:, cz + 1, own, :], init_send.at[3], init_recv.at[3], d_dn, p
        ),
        remote(spk.at[0], sigp.at[1], init_send.at[4], init_recv.at[4], d, p_dn),
        remote(spk.at[1], sigp.at[0], init_send.at[5], init_recv.at[5], d, p_up),
        remote(flags.at[cz - 1], flg.at[0], init_send.at[6], init_recv.at[6], d_up, p),
        remote(flags.at[0], flg.at[cz + 1], init_send.at[7], init_recv.at[7], d_dn, p),
    ]
    for copy in init:
        copy.start()

    for i in (1, 2, 4, 5, 6, 7, 8):
        local[i].wait()

    def tables(i, unused):
        at = pl.ds(pl.multiple_of(i * chunk, chunk), chunk)
        cell = cellv[:, at]
        elem = elemv[:, at]
        live = cell >= 0
        c_row = jnp.where(live, cell // cy, -1)
        c_col = jnp.where(live, cell % cy, -1)
        block = elem // (tiles * 1024)
        inner = elem - block * (tiles * 1024)
        half_row = inner // 128
        p_row = block * block_rows + (half_row // 16) * 8 + half_row % 8
        p_col = (half_row // 8 % 2) * 128 + inner % 128
        p_row = jnp.where(live, p_row, -1)
        crow[:, at] = c_row
        prow[:, at] = p_row
        across = lax.broadcasted_iota(jnp.int32, (cy, chunk), 0)
        acol[:, at] = (across == c_col).astype(F32).astype(BF16)
        arow[:, at] = (across[:rows] == c_row).astype(F32).astype(BF16)
        wide = lax.broadcasted_iota(jnp.int32, (256, chunk), 0)
        bcol[:, at] = (wide == p_col).astype(F32).astype(BF16)
        brow[:, at] = (wide[:prows] == p_row).astype(F32).astype(BF16)
        return unused

    lax.fori_loop(0, pairs // chunk, tables, 0)

    def split_start(z, unused):
        for c in range(3):
            high, low = split_two(v0[c, z])
            at = pl.ds(pl.multiple_of(c * rows + z * cx, 16), cx)
            thi[at, :] = high
            tlo[at, :] = low
        scale[z] = DT / scale[z]
        return unused

    lax.fori_loop(0, cz, split_start, 0)
    def pile_terms(s):
        acc_s[...] = jnp.zeros_like(acc_s)

        def body(i, unused):
            at = pl.ds(pl.multiple_of(i * chunk, chunk), chunk)
            col = acol[:, at]
            picked = dot_nn(thi[...], col) + dot_nn(tlo[...], col)
            here = lax.broadcasted_iota(jnp.int32, (rows, chunk), 0) == crow[:, at]
            row = brow[:, at]
            high, low = [], []
            for c in range(3):
                value = jnp.sum(
                    jnp.where(here, picked[c * rows : (c + 1) * rows], 0.0), axis=0, keepdims=True
                )
                first, second = split_two(value)
                high.append(row * first)
                low.append(row * second)
            wide = bcol[:, at]
            acc_s[...] += dot_nt(jnp.concatenate(high, 0), wide) + dot_nt(
                jnp.concatenate(low, 0), wide
            )
            return unused

        lax.fori_loop(0, pairs // chunk, body, 0)
        for b in range(3):
            for c in range(3):
                for t in range(tiles):
                    r = c * prows + b * block_rows + t // 2 * 8
                    l = t % 2 * 128
                    value = acc_s[r : r + 8, l : l + 128]
                    if s == 0:
                        value = value - sbuf[0, b, units + t] * pvw[0, b, c * tiles + t]
                    sbuf[s, b, c * tiles + t] = value

    def cell_terms(s):
        acc_c[...] = jnp.zeros_like(acc_c)
        for b in range(3):
            for c in range(3):
                for a in range(tiles // 2):
                    u = c * tiles + 2 * a
                    r = c * prows + b * block_rows + a * 8
                    phi[r : r + 8, 0:128] = pvw[s, b, u]
                    phi[r : r + 8, 128:256] = pvw[s, b, u + 1]
        high, low = split_two(phi[...])
        plo[0] = high
        plo[1] = low

        def body(i, unused):
            at = pl.ds(pl.multiple_of(i * chunk, chunk), chunk)
            col = bcol[:, at]
            picked = dot_nn(plo[0], col) + dot_nn(plo[1], col)
            here = lax.broadcasted_iota(jnp.int32, (prows, chunk), 0) == prow[:, at]
            row = arow[:, at]
            high, low = [], []
            for c in range(3):
                value = jnp.sum(
                    jnp.where(here, picked[c * prows : (c + 1) * prows], 0.0),
                    axis=0,
                    keepdims=True,
                )
                first, second = split_two(value)
                high.append(row * first)
                low.append(row * second)
            wide = acol[:, at]
            acc_c[...] += dot_nt(jnp.concatenate(high, 0), wide) + dot_nt(
                jnp.concatenate(low, 0), wide
            )
            return unused

        lax.fori_loop(0, pairs // chunk, body, 0)

    count_c[...] = dot_nt(arow[...], acol[...])
    acc_s[0:prows, :] = dot_nt(brow[...], bcol[...])
    for b in range(3):
        for t in range(tiles):
            r = b * block_rows + t // 2 * 8
            l = t % 2 * 128
            sbuf[0, b, units + t] = acc_s[r : r + 8, l : l + 128]
    phi[...] = jnp.zeros_like(phi)
    init[0].wait_recv()
    init[1].wait_recv()

    def depth_leg(s):
        many = pl.ds(0, units + tiles if s == 0 else units)
        return [
            remote(
                sbuf.at[s, 0, many],
                sdep.at[s, 1, many],
                dep_send.at[s, 0],
                dep_recv.at[s, 0],
                d_dn,
                p,
            ),
            remote(
                sbuf.at[s, 2, many],
                sdep.at[s, 0, many],
                dep_send.at[s, 1],
                dep_recv.at[s, 1],
                d_up,
                p,
            ),
        ]

    def start_parts(s):
        many = units + tiles if s == 0 else units
        for u in range(many):
            sown[s, u] = sbuf[s, 1, u] + sdep[s, 0, u] + sdep[s, 1, u]

        def go(j, number):
            def body(k, unused):
                q = lax.rem(p + k, plan_count)
                u = q + plan_count * j

                def send():
                    if number:
                        remote(
                            sown.at[0, units + lax.rem(u, tiles)],
                            rxn.at[j, p],
                            num_send.at[j],
                            num_recv.at[j],
                            d,
                            q,
                        ).start()
                    else:
                        remote(
                            sown.at[s, u],
                            rx.at[s, j, p],
                            part_send.at[s, j],
                            part_recv.at[s, j],
                            d,
                            q,
                        ).start()

                if plan_count * (j + 1) <= units:
                    send()
                else:
                    pl.when(u < units)(send)
                return unused

            lax.fori_loop(1, plan_count, body, 0)

        for j in range(slots):
            go(j, False)
        if s == 0:
            for j in range(slots):
                go(j, True)

    def owners(j, work):
        if plan_count * (j + 1) <= units:
            work()
        else:
            pl.when(p + plan_count * j < units)(work)

    def total(get):
        value = get(0)
        for i in range(1, plan_count):
            value = value + get(i)
        return value

    def update_pile(s):
        for j in range(slots):
            u = p + plan_count * j

            def work():
                t = lax.rem(u, tiles)
                most = pl.ds(0, plan_count - 1)
                remote(
                    rx.at[s, j, most],
                    rx.at[s, j, most],
                    part_send.at[s, j],
                    part_recv.at[s, j],
                    d,
                    p_up,
                ).wait_recv()
                rx[s, j, p] = sown[s, u]
                if s == 0:
                    remote(
                        rxn.at[j, most],
                        rxn.at[j, most],
                        num_send.at[j],
                        num_recv.at[j],
                        d,
                        p_up,
                    ).wait_recv()
                    rxn[j, p] = sown[0, units + t]
                    nown[j] = total(lambda i: rxn[j, i])
                force = jackv[u] + total(lambda i: rx[s, j, i])
                before = pvw[s, 1, u]
                if s > 0:
                    force = force - nown[j] * before
                pvw[s + 1, 1, u] = before + DT * force / massv[t]

                def body(k, unused):
                    remote(
                        pvw.at[s + 1, 1, u],
                        pvw.at[s + 1, 1, u],
                        all_send.at[s, j],
                        all_recv.at[s, j],
                        d,
                        lax.rem(p + k, plan_count),
                    ).start()
                    return unused

                lax.fori_loop(1, plan_count, body, 0)

            owners(j, work)

    def wait_pile(s):
        for j in range(slots):
            here = min(plan_count, units - plan_count * j)

            def take(number):
                if number > 0:
                    some = pl.ds(0, number)
                    remote(
                        pvw.at[s + 1, 1, some],
                        pvw.at[s + 1, 1, some],
                        all_send.at[s, j],
                        all_recv.at[s, j],
                        d,
                        p_up,
                    ).wait_recv()

            if here == plan_count:
                take(here - 1)
            else:
                pl.when(p < here)(lambda: take(here - 1))
                pl.when(p >= here)(lambda: take(here))

    def window_leg(s):
        return [
            remote(
                pvw.at[s, 1], pvw.at[s, 0], win_send.at[s - 1, 0], win_recv.at[s - 1, 0], d_up, p
            ),
            remote(
                pvw.at[s, 1], pvw.at[s, 2], win_send.at[s - 1, 1], win_recv.at[s - 1, 1], d_dn, p
            ),
        ]

    lane = lax.broadcasted_iota(jnp.int32, (cx, cy), 1)
    lane_p = lax.broadcasted_iota(jnp.int32, (cz, cy), 1)

    def new_velocity(s):
        def body(z, unused):
            for c in (1, 3, 5):
                sig[c, z + 1, 7:8, :] = sigp[0, c, pl.ds(z, 1), :]
                sig[c, z + 1, cx + 8 : cx + 9, :] = sigp[1, c, pl.ds(z, 1), :]
            for c in range(3):
                i, j, k = SYM[c]
                force = sig[i, z + 2, own, :] - sig[i, z, own, :]
                force += sig[j, z + 1, pl.ds(9, cx), :] - sig[j, z + 1, pl.ds(7, cx), :]
                force += along_y(sig[k, z + 1, own, :], lane, cy)
                old = v0[c, z] if s == 0 else vx[s - 1, c, z + 2, own, :]
                at = pl.ds(pl.multiple_of(z * cx, 16), cx)
                spot = pl.ds(pl.multiple_of(c * rows + z * cx, 16), cx)
                push = acc_c[spot, :] - count_c[at, :] * old
                new = old + scale[z] * (0.5 * force + push)
                vx[s, c, z + 2, own, :] = new
                if s < STEPS - 1:
                    high, low = split_two(new)
                    thi[spot, :] = high
                    tlo[spot, :] = low
                row = pl.ds(z, 1)
                pbuf[s, 0, c, 0, row, :] = new[0:1]
                pbuf[s, 1, c, 1, row, :] = new[cx - 1 : cx]
                if s < STEPS - 1:
                    pbuf[s, 0, c, 1, row, :] = new[1:2]
                    pbuf[s, 1, c, 0, row, :] = new[cx - 2 : cx - 1]
            return unused

        lax.fori_loop(0, cz, body, 0)
        if s < STEPS - 1:
            for i in range(4):
                z = cz - 1 if i // 2 else 0
                x = cx - 1 if i % 2 else 0
                for c in range(3):
                    cbuf[s, i, c : c + 1, :] = vx[s, c, z + 2, 8 + x : 9 + x, :]

    def halo_leg(s):
        w = 2 if s < STEPS - 1 else 1
        xs0 = pl.ds(0, w)
        xs1 = pl.ds(2 - w, w)
        mid = pl.ds(8, cz)
        send = lambda i: (halo_send.at[s, i], halo_recv.at[s, i])
        copies = [
            remote(
                vx.at[s, :, pl.ds(cz + 2 - w, w), own, :],
                vx.at[s, :, pl.ds(2 - w, w), own, :],
                *send(0),
                d_up,
                p,
            ),
            remote(
                vx.at[s, :, pl.ds(2, w), own, :],
                vx.at[s, :, pl.ds(cz + 2, w), own, :],
                *send(1),
                d_dn,
                p,
            ),
            remote(pbuf.at[s, 0, :, xs0], rxp.at[s, 1, :, xs0, mid, :], *send(2), d, p_dn),
            remote(pbuf.at[s, 1, :, xs1], rxp.at[s, 0, :, xs1, mid, :], *send(3), d, p_up),
        ]
        if s < STEPS - 1:
            for i in range(4):
                copies.append(remote(cbuf.at[s, i], crx.at[s, i], *send(4 + i), *corners[i]))
        return copies

    def new_stress(s):
        last = s == STEPS - 1

        @pl.when(d == 0)
        def _():
            vx[s, :, 0:2, own, :] = jnp.zeros((3, 2, cx, cy), F32)
            if not last:
                crx[s, 2:4] = jnp.zeros((2, 3, cy), F32)

        @pl.when(d == depth_count - 1)
        def _():
            vx[s, :, cz + 2 : cz + 4, own, :] = jnp.zeros((3, 2, cx, cy), F32)
            if not last:
                crx[s, 0:2] = jnp.zeros((2, 3, cy), F32)

        @pl.when(p == 0)
        def _():
            rxp[s, 0, :, :, 8 : 8 + cz, :] = jnp.zeros((3, 2, cz, cy), F32)
            if not last:
                for i in (1, 3):
                    crx[s, i] = jnp.zeros((3, cy), F32)

        @pl.when(p == plan_count - 1)
        def _():
            rxp[s, 1, :, :, 8 : 8 + cz, :] = jnp.zeros((3, 2, cz, cy), F32)
            if not last:
                for i in (0, 2):
                    crx[s, i] = jnp.zeros((3, cy), F32)

        if not last:
            for c in range(3):
                for side in range(2):
                    x = 7 if side == 0 else cx + 8
                    below = crx[s, 3 - side, c : c + 1, :]
                    above = crx[s, 1 - side, c : c + 1, :]
                    vx[s, c, 1, x : x + 1, :] = below
                    vx[s, c, cz + 2, x : x + 1, :] = above
                    rxp[s, side, c, 1 - side, 7:8, :] = below
                    rxp[s, side, c, 1 - side, cz + 8 : cz + 9, :] = above

        def rows_in(z, unused):
            for c in range(3):
                vx[s, c, z + 2, 7:8, :] = rxp[s, 0, c, 1, pl.ds(z + 8, 1), :]
                vx[s, c, z + 2, cx + 8 : cx + 9, :] = rxp[s, 1, c, 0, pl.ds(z + 8, 1), :]
            return unused

        lax.fori_loop(0, cz, rows_in, 0)

        def body(layer, unused):
            dz = [
                vx[s, c, layer + 2, own, :] - vx[s, c, layer, own, :] for c in range(3)
            ]
            dx = [
                vx[s, c, layer + 1, pl.ds(9, cx), :] - vx[s, c, layer + 1, pl.ds(7, cx), :]
                for c in range(3)
            ]
            dy = [along_y(vx[s, c, layer + 1, own, :], lane, cy) for c in range(3)]
            flag = flg[layer]
            new = updated_stress(
                [sig[c, layer, own, :] for c in range(6)], dz, dx, dy, flag == 0, flag == 1
            )
            for c in range(6):
                sig[c, layer, own, :] = new[c]
            return unused

        if last:
            lax.fori_loop(1, cz + 1, body, 0)
            return
        lax.fori_loop(0, cz + 2, body, 0)
        for side in range(2):
            inner = [pbuf[s, side, c, side] for c in range(3)]
            outer = [rxp[s, side, c, side, 8 : 8 + cz, :] for c in range(3)]
            sign = 1.0 if side == 0 else -1.0
            ring = 1 - side
            dz = [
                rxp[s, side, c, ring, 9 : 9 + cz, :] - rxp[s, side, c, ring, 7 : 7 + cz, :]
                for c in range(3)
            ]
            dx = [sign * (inner[c] - outer[c]) for c in range(3)]
            dy = [along_y(rxp[s, side, c, ring, 8 : 8 + cz, :], lane_p, cy) for c in range(3)]
            flag = sigp[side, 6]
            new = updated_stress(
                [sigp[side, c] for c in range(6)], dz, dx, dy, flag == 0.0, flag == 1.0
            )
            for c in range(6):
                sigp[side, c] = new[c]
        clear_outside()

    def clear_outside():
        @pl.when(d == 0)
        def _():
            sig[:, 0, own, :] = jnp.zeros((6, cx, cy), F32)

        @pl.when(d == depth_count - 1)
        def _():
            sig[:, cz + 1, own, :] = jnp.zeros((6, cx, cy), F32)

        @pl.when(p == 0)
        def _():
            sigp[0, 0:6] = jnp.zeros((6, cz, cy), F32)

        @pl.when(p == plan_count - 1)
        def _():
            sigp[1, 0:6] = jnp.zeros((6, cz, cy), F32)

    def start(copies):
        for copy in copies:
            copy.start()
        return copies

    def arrive(copies):
        for copy in copies:
            copy.wait_recv()

    pile_terms(0)
    legs = [start(depth_leg(0))]
    cell_terms(0)
    arrive(legs[0])
    start_parts(0)
    arrive(init[2:])
    clear_outside()
    new_velocity(0)
    halos = [start(halo_leg(0))]
    pile_terms(1)
    legs.append(start(depth_leg(1)))
    update_pile(0)
    arrive(halos[0])
    new_stress(0)
    arrive(legs[1])
    start_parts(1)
    wait_pile(0)
    windows = [start(window_leg(1))]
    arrive(windows[0])
    cell_terms(1)
    new_velocity(1)
    halos.append(start(halo_leg(1)))
    pile_terms(2)
    legs.append(start(depth_leg(2)))
    update_pile(1)
    arrive(halos[1])
    new_stress(1)
    arrive(legs[2])
    start_parts(2)
    wait_pile(1)
    windows.append(start(window_leg(2)))
    arrive(windows[1])
    cell_terms(2)
    new_velocity(2)
    halos.append(start(halo_leg(2)))
    velocity_back = pltpu.make_async_copy(
        vx.at[2, :, pl.ds(2, cz), own, :], velocity_out, local_sem.at[0]
    )
    velocity_back.start()
    update_pile(2)
    arrive(halos[2])
    new_stress(2)
    stress_back = pltpu.make_async_copy(
        sig.at[:, pl.ds(1, cz), own, :], stress_out, local_sem.at[1]
    )
    stress_back.start()
    wait_pile(2)
    pile_back = pltpu.make_async_copy(pvw.at[3, 1], pile_out, local_sem.at[2])
    pile_back.start()

    for copies in [init] + halos + legs + windows:
        for copy in copies:
            copy.wait_send()
    for s in range(STEPS):
        for j in range(slots):
            here = min(plan_count, units - plan_count * j)

            def gone(number):
                if number > 0:
                    some = pl.ds(0, number)
                    remote(
                        rx.at[s, j, some],
                        rx.at[s, j, some],
                        part_send.at[s, j],
                        part_recv.at[s, j],
                        d,
                        p_up,
                    ).wait_send()
                    if s == 0:
                        remote(
                            rxn.at[j, some],
                            rxn.at[j, some],
                            num_send.at[j],
                            num_recv.at[j],
                            d,
                            p_up,
                        ).wait_send()

            if here == plan_count:
                gone(here - 1)
            else:
                pl.when(p < here)(lambda: gone(here - 1))
                pl.when(p >= here)(lambda: gone(here))

            def spread():
                most = pl.ds(0, plan_count - 1)
                remote(
                    rx.at[s, j, most],
                    rx.at[s, j, most],
                    all_send.at[s, j],
                    all_recv.at[s, j],
                    d,
                    p_up,
                ).wait_send()

            owners(j, spread)
    velocity_back.wait()
    stress_back.wait()
    pile_back.wait()


def shards(
    depth_count,
    plan_count,
    stress,
    velocity,
    density,
    flags,
    pile_velocity,
    pile_mass,
    jack_force,
    pair_elem,
    pair_cell,
):
    cz, cx, cy = density.shape
    width = pile_mass.shape[0]
    tiles = width // 1024
    pairs = pair_elem.shape[1]
    chunk = min(512, pairs)
    units = 3 * tiles
    slots = -(-units // plan_count)
    rows = cz * cx
    prows = -(-(3 * width // 256) // 16) * 16
    sizes = (depth_count, plan_count, cz, cx, cy, tiles, pairs, chunk)
    vm = lambda *shape: pltpu.VMEM(shape, F32)
    half = lambda *shape: pltpu.VMEM(shape, BF16)
    whole = lambda *shape: pltpu.VMEM(shape, jnp.int32)
    dma = lambda *shape: pltpu.SemaphoreType.DMA(shape)
    scratch = [
        vm(6, cz + 2, cx + 16, cy),
        vm(STEPS, 3, cz + 4, cx + 16, cy),
        vm(3, cz, cx, cy),
        vm(cz, cx, cy),
        whole(cz + 2, cx, cy),
        vm(2, 7, cz, cy),
        vm(2, 7, cz, cy),
        vm(STEPS, 2, 3, 2, cz, cy),
        vm(STEPS, 2, 3, 2, cz + 16, cy),
        vm(STEPS, 4, 3, cy),
        vm(STEPS, 4, 3, cy),
        vm(STEPS + 1, 3, units, 8, 128),
        vm(tiles, 8, 128),
        vm(units, 8, 128),
        whole(1, pairs),
        whole(1, pairs),
        whole(1, pairs),
        whole(1, pairs),
        half(cy, pairs),
        half(rows, pairs),
        half(256, pairs),
        half(prows, pairs),
        half(3 * rows, cy),
        half(3 * rows, cy),
        vm(3 * prows, 256),
        half(2, 3 * prows, 256),
        vm(3 * prows, 256),
        vm(3 * rows, cy),
        vm(rows, cy),
        vm(STEPS, 3, units + tiles, 8, 128),
        vm(STEPS, 2, units + tiles, 8, 128),
        vm(STEPS, units + tiles, 8, 128),
        vm(STEPS, slots, plan_count, 8, 128),
        vm(slots, plan_count, 8, 128),
        vm(slots, 8, 128),
        dma(9),
        dma(8),
        dma(8),
        dma(STEPS, 8),
        dma(STEPS, 8),
        dma(STEPS, 2),
        dma(STEPS, 2),
        dma(STEPS, slots),
        dma(STEPS, slots),
        dma(slots),
        dma(slots),
        dma(STEPS, slots),
        dma(STEPS, slots),
        dma(STEPS - 1, 2),
        dma(STEPS - 1, 2),
    ]
    anywhere = pl.BlockSpec(memory_space=pl.ANY)
    stress, velocity, pile = pl.pallas_call(
        functools.partial(kernel, sizes),
        out_shape=(
            jax.ShapeDtypeStruct(stress.shape, F32),
            jax.ShapeDtypeStruct(velocity.shape, F32),
            jax.ShapeDtypeStruct((units, 8, 128), F32),
        ),
        in_specs=[anywhere] * 9,
        out_specs=(anywhere,) * 3,
        scratch_shapes=scratch,
        compiler_params=pltpu.CompilerParams(
            collective_id=0, has_side_effects=True, vmem_limit_bytes=40 * 1024 * 1024
        ),
    )(
        stress,
        velocity,
        density,
        flags,
        pile_velocity.reshape(units, 8, 128),
        pile_mass.reshape(tiles, 8, 128),
        jack_force.reshape(units, 8, 128),
        pair_elem,
        pair_cell,
    )
    return stress, velocity, pile.reshape(3, width)


def solution(mesh):
    field = P(None, "depth", "plan", None)
    cells = P("depth", "plan", None)
    placed = (
        field,
        field,
        cells,
        cells,
        P(None, "depth"),
        P("depth"),
        P(None, "depth"),
        P("depth", "plan"),
        P("depth", "plan"),
    )
    return jax.shard_map(
        functools.partial(shards, mesh.shape["depth"], mesh.shape["plan"]),
        mesh=mesh,
        in_specs=placed,
        out_specs=(field, field, P(None, "depth")),
        check_vma=False,
    )
```

```python
import functools

import jax
import jax.numpy as jnp
from jax import lax
from jax.experimental import pallas as pl
from jax.experimental.pallas import tpu as pltpu
from jax.sharding import PartitionSpec as P

STEPS = 3
DT = 0.2
MESH = pl.DeviceIdType.MESH
F32 = jnp.float32
BF16 = jnp.bfloat16
SYM = ((0, 3, 4), (3, 1, 5), (4, 5, 2))
HALF_ROWS = 8


def split_two(x):
    high = x.astype(BF16)
    return high, (x - high.astype(F32)).astype(BF16)


def dot_nn(a, b):
    return jnp.dot(a, b, preferred_element_type=F32)


def dot_nt(a, b):
    return lax.dot_general(a, b, (((1,), (1,)), ((), ())), preferred_element_type=F32)


def along_y(a, lane, width):
    after = jnp.where(lane < width - 1, pltpu.roll(a, width - 1, 1), 0.0)
    before = jnp.where(lane > 0, pltpu.roll(a, 1, 1), 0.0)
    return after - before


def updated_stress(sig, dz, dx, dy, elastic, cone):
    half = 0.5 * DT
    common = half * (dz[0] + dx[1] + dy[2])
    trial = [
        sig[0] + DT * dz[0] + common,
        sig[1] + DT * dx[1] + common,
        sig[2] + DT * dy[2] + common,
        sig[3] + half * (dx[0] + dz[1]),
        sig[4] + half * (dy[0] + dz[2]),
        sig[5] + half * (dy[1] + dx[2]),
    ]
    pressure = (trial[0] + trial[1] + trial[2]) * (1.0 / 3.0)
    dev = [trial[i] - pressure for i in range(3)]
    second = 0.5 * (dev[0] * dev[0] + dev[1] * dev[1] + dev[2] * dev[2]) + (
        trial[3] * trial[3] + trial[4] * trial[4] + trial[5] * trial[5]
    )
    shrink = 1.0 / (1.0 + 1.5 * jnp.sqrt(second))
    factor = jnp.where(elastic, 1.0, jnp.where(cone, shrink, 0.0))
    new = [dev[i] * factor + pressure for i in range(3)]
    return new + [trial[i] * factor for i in range(3, 6)]


def kernel(
    sizes,
    stress,
    velocity,
    density,
    flags,
    pile0,
    mass,
    jack,
    pair_elem,
    pair_cell,
    stress_out,
    velocity_out,
    pile_out,
    sig,
    vx,
    v0,
    scale,
    flg,
    sigp,
    spk,
    pbuf,
    rxp,
    cbuf,
    crx,
    pvw,
    massv,
    jackv,
    pilev,
    jackw,
    elemv,
    cellv,
    crow,
    prow,
    acol,
    arow,
    bcol,
    brow,
    thi,
    tlo,
    phi,
    plo,
    acc_s,
    acc_c,
    count_c,
    sbuf,
    rx,
    nbuf,
    ndep,
    nsum,
    rxn,
    nown,
    local_sem,
    init_send,
    init_recv,
    halo_send,
    halo_recv,
    dep_send,
    dep_recv,
    part_send,
    part_recv,
    num_send,
    num_recv,
    all_send,
    all_recv,
):
    depth_count, plan_count, cz, cx, cy, tiles, pairs, chunk = sizes
    units = 3 * tiles
    slots = -(-units // plan_count)
    rows = cz * cx
    prows = brow.shape[0]
    block_rows = tiles // 2 * 8
    d = lax.axis_index("depth")
    p = lax.axis_index("plan")
    d_up = lax.rem(d + 1, depth_count)
    d_dn = lax.rem(d + depth_count - 1, depth_count)
    p_up = lax.rem(p + 1, plan_count)
    p_dn = lax.rem(p + plan_count - 1, plan_count)
    own = pl.ds(8, cx)
    y_count = plan_count // 2
    y = p // 2
    z_low = p % 2
    odd = d % 2
    d_near = d + 1 - 2 * odd
    d_far = lax.rem(d + depth_count - 1 + 2 * odd, depth_count)
    kinds = ((d_far, 2 * odd), (d_near, 2 - 2 * odd), (d, 1))

    def everyone(first, visit):
        def body(i, unused):
            step = (i + 1) // 2
            yy = lax.rem(y + y_count // 2 + step * (1 - 2 * (i % 2)) + y_count, y_count)
            for kind in range(first, 3):
                dd, block = kinds[kind]
                for z in (1 - z_low, z_low):
                    act = functools.partial(visit, kind, dd, block, yy * 2 + z)
                    if kind == 2 and z is z_low:
                        pl.when(i < y_count - 1)(act)
                    else:
                        act()
            return unused

        lax.fori_loop(0, y_count, body, 0)

    def remote(src, dst, send, recv, dd, pp):
        return pltpu.make_async_remote_copy(
            src_ref=src,
            dst_ref=dst,
            send_sem=send,
            recv_sem=recv,
            device_id={"depth": dd, "plan": pp},
            device_id_type=MESH,
        )

    local = [
        (stress, sig.at[:, pl.ds(1, cz), own, :]),
        (velocity, v0),
        (density, scale),
        (flags, flg.at[pl.ds(1, cz)]),
        (pile0, pilev),
        (mass, massv),
        (jack, jackw),
        (pair_elem, elemv),
        (pair_cell, cellv),
    ]
    local = [
        pltpu.make_async_copy(src, dst, local_sem.at[i]) for i, (src, dst) in enumerate(local)
    ]
    for copy in local:
        copy.start()

    barrier = pltpu.get_barrier_semaphore()
    corners = ((d_dn, p_dn), (d_dn, p_up), (d_up, p_dn), (d_up, p_up))

    def greet(kind, dd, block, q):
        pl.semaphore_signal(
            barrier, inc=1, device_id={"depth": dd, "plan": q}, device_id_type=MESH
        )

    everyone(0, greet)
    for i in (0, 3):
        local[i].wait()

    def pack_edges(z, unused):
        at = pl.ds(z, 1)
        for c in range(6):
            spk[0, c, at, :] = sig[c, z + 1, 8:9, :]
            spk[1, c, at, :] = sig[c, z + 1, cx + 7 : cx + 8, :]
        spk[0, 6, at, :] = flg[z + 1, 0:1, :].astype(F32)
        spk[1, 6, at, :] = flg[z + 1, cx - 1 : cx, :].astype(F32)
        return unused

    lax.fori_loop(0, cz, pack_edges, 0)

    local[4].wait()
    local[6].wait()

    def pile_tiles(t, unused):
        for r in range(8):
            at = pl.ds(pl.multiple_of(t * 1024 + r * 128, 128), 128)
            for source, target, first in ((pilev, pvw.at[0], units), (jackw, jackv, 0)):
                value = source[:, at]
                for c in range(3):
                    target[first + c * tiles + t, r : r + 1, :] = value[c : c + 1]
        return unused

    lax.fori_loop(0, tiles, pile_tiles, 0)
    for i in (1, 2, 5, 7, 8):
        local[i].wait()

    def tables(i, unused):
        at = pl.ds(pl.multiple_of(i * chunk, chunk), chunk)
        cell = cellv[:, at]
        elem = elemv[:, at]
        live = cell >= 0
        c_row = jnp.where(live, cell // cy, -1)
        c_col = jnp.where(live, cell % cy, -1)
        block = elem // (tiles * 1024)
        inner = elem - block * (tiles * 1024)
        half_row = inner // 128
        p_row = block * block_rows + (half_row // 16) * 8 + half_row % 8
        p_col = (half_row // 8 % 2) * 128 + inner % 128
        p_row = jnp.where(live, p_row, -1)
        crow[:, at] = c_row
        prow[:, at] = p_row
        across = lax.broadcasted_iota(jnp.int32, (cy, chunk), 0)
        acol[:, at] = (across == c_col).astype(F32).astype(BF16)
        arow[:, at] = (across[:rows] == c_row).astype(F32).astype(BF16)
        wide = lax.broadcasted_iota(jnp.int32, (256, chunk), 0)
        bcol[:, at] = (wide == p_col).astype(F32).astype(BF16)
        brow[:, at] = (wide[:prows] == p_row).astype(F32).astype(BF16)
        return unused

    lax.fori_loop(0, pairs // chunk, tables, 0)

    def split_start(z, unused):
        for c in range(3):
            high, low = split_two(v0[c, z])
            at = pl.ds(pl.multiple_of(c * rows + z * cx, 16), cx)
            thi[at, :] = high
            tlo[at, :] = low
        scale[z] = DT / scale[z]
        return unused

    lax.fori_loop(0, cz, split_start, 0)
    def pile_terms(s):
        acc_s[...] = jnp.zeros_like(acc_s)

        def body(i, unused):
            at = pl.ds(pl.multiple_of(i * chunk, chunk), chunk)
            col = acol[:, at]
            picked = dot_nn(thi[...], col) + dot_nn(tlo[...], col)
            here = lax.broadcasted_iota(jnp.int32, (rows, chunk), 0) == crow[:, at]
            row = brow[:, at]
            high, low = [], []
            for c in range(3):
                value = jnp.sum(
                    jnp.where(here, picked[c * rows : (c + 1) * rows], 0.0), axis=0, keepdims=True
                )
                first, second = split_two(value)
                high.append(row * first)
                low.append(row * second)
            wide = bcol[:, at]
            acc_s[...] += dot_nt(jnp.concatenate(high, 0), wide) + dot_nt(
                jnp.concatenate(low, 0), wide
            )
            return unused

        lax.fori_loop(0, pairs // chunk, body, 0)
        for b in range(3):
            for c in range(3):
                for t in range(tiles):
                    r = c * prows + b * block_rows + t // 2 * 8
                    l = t % 2 * 128
                    sbuf[s, b, c * tiles + t] = acc_s[r : r + 8, l : l + 128]

    def cell_terms(s):
        acc_c[...] = jnp.zeros_like(acc_c)
        for b in range(3):
            for c in range(3):
                for a in range(tiles // 2):
                    u = b * units + c * tiles + 2 * a
                    r = c * prows + b * block_rows + a * 8
                    phi[r : r + 8, 0:128] = pvw[s, u]
                    phi[r : r + 8, 128:256] = pvw[s, u + 1]
        high, low = split_two(phi[...])
        plo[0] = high
        plo[1] = low

        def body(i, unused):
            at = pl.ds(pl.multiple_of(i * chunk, chunk), chunk)
            col = bcol[:, at]
            picked = dot_nn(plo[0], col) + dot_nn(plo[1], col)
            here = lax.broadcasted_iota(jnp.int32, (prows, chunk), 0) == prow[:, at]
            row = arow[:, at]
            high, low = [], []
            for c in range(3):
                value = jnp.sum(
                    jnp.where(here, picked[c * prows : (c + 1) * prows], 0.0),
                    axis=0,
                    keepdims=True,
                )
                first, second = split_two(value)
                high.append(row * first)
                low.append(row * second)
            wide = acol[:, at]
            acc_c[...] += dot_nt(jnp.concatenate(high, 0), wide) + dot_nt(
                jnp.concatenate(low, 0), wide
            )
            return unused

        lax.fori_loop(0, pairs // chunk, body, 0)

    count_c[...] = dot_nt(arow[...], acol[...])
    acc_s[0:prows, :] = dot_nt(brow[...], bcol[...])
    for b in range(3):
        for t in range(tiles):
            r = b * block_rows + t // 2 * 8
            l = t % 2 * 128
            nbuf[b, t] = acc_s[r : r + 8, l : l + 128]
    phi[...] = jnp.zeros_like(phi)
    pl.semaphore_wait(barrier, 3 * plan_count - 1)
    mine = pl.ds(units, units)
    init = [
        remote(
            nbuf.at[0], ndep.at[1], dep_send.at[0], dep_recv.at[0], d_dn, p
        ),
        remote(
            nbuf.at[2], ndep.at[0], dep_send.at[1], dep_recv.at[1], d_up, p
        ),
        remote(
            pvw.at[0, mine],
            pvw.at[0, pl.ds(0, units)],
            init_send.at[0],
            init_recv.at[0],
            d_up,
            p,
        ),
        remote(
            pvw.at[0, mine],
            pvw.at[0, pl.ds(2 * units, units)],
            init_send.at[1],
            init_recv.at[1],
            d_dn,
            p,
        ),
        remote(
            stress.at[:, cz - 1], sig.at[:, 0, own, :], init_send.at[2], init_recv.at[2], d_up, p
        ),
        remote(
            stress.at[:, 0], sig.at[:, cz + 1, own, :], init_send.at[3], init_recv.at[3], d_dn, p
        ),
        remote(spk.at[0], sigp.at[1], init_send.at[4], init_recv.at[4], d, p_dn),
        remote(spk.at[1], sigp.at[0], init_send.at[5], init_recv.at[5], d, p_up),
        remote(flags.at[cz - 1], flg.at[0], init_send.at[6], init_recv.at[6], d_up, p),
        remote(flags.at[0], flg.at[cz + 1], init_send.at[7], init_recv.at[7], d_dn, p),
    ]
    for copy in init:
        copy.start()

    def owned(j, q, work):
        if plan_count * (j + 1) <= units:
            work()
        else:
            pl.when(q + plan_count * j < units)(work)

    def start_parts(s):
        def visit(kind, dd, block, q):
            for j in range(slots):
                owned(
                    j,
                    q,
                    lambda: remote(
                        sbuf.at[s, block, q + plan_count * j],
                        rx.at[s, j, kind * plan_count + p],
                        part_send.at[s, j],
                        part_recv.at[s, j],
                        dd,
                        q,
                    ).start(),
                )

        everyone(0, visit)

    def start_numbers():
        for t in range(tiles):
            nsum[t] = nbuf[1, t] + ndep[0, t] + ndep[1, t]

        def visit(kind, dd, block, q):
            for j in range(slots):
                owned(
                    j,
                    q,
                    lambda: remote(
                        nsum.at[lax.rem(q + plan_count * j, tiles)],
                        rxn.at[j, p],
                        num_send.at[j],
                        num_recv.at[j],
                        d,
                        q,
                    ).start(),
                )

        everyone(2, visit)

    def some_of(ref, number, send, recv):
        some = ref.at[pl.ds(0, number)]
        return remote(some, some, send, recv, d, p_up)

    def parts_wait(s, j, number):
        return some_of(rx.at[s, j], number, part_send.at[s, j], part_recv.at[s, j])

    def numbers_wait(j, number):
        return some_of(rxn.at[j], number, num_send.at[j], num_recv.at[j])

    def all_wait(s, j, number):
        return some_of(pvw.at[s + 1], number, all_send.at[s, j], all_recv.at[s, j])

    def not_mine(j, many, act):
        here = min(plan_count, units - plan_count * j)
        if here == plan_count:
            act(here * many - 1)
        else:
            if here * many > 1:
                pl.when(p < here)(lambda: act(here * many - 1))
            pl.when(p >= here)(lambda: act(here * many))

    def update_pile(s):
        first = 0 if s < STEPS - 1 else 2
        for j in range(slots):
            u = p + plan_count * j

            def work():
                t = lax.rem(u, tiles)
                parts_wait(s, j, 3 * plan_count - 1).wait_recv()
                rx[s, j, 2 * plan_count + p] = sbuf[s, 1, u]
                if s == 0:
                    numbers_wait(j, plan_count - 1).wait_recv()
                    rxn[j, p] = nsum[t]
                    nown[j] = jnp.sum(rxn[j], axis=0)
                before = pvw[s, units + u]
                force = jackv[u] + jnp.sum(rx[s, j], axis=0) - nown[j] * before
                pvw[s + 1, units + u] = before + DT * force / massv[t]

                def visit(kind, dd, block, q):
                    remote(
                        pvw.at[s + 1, units + u],
                        pvw.at[s + 1, (2 - block) * units + u],
                        all_send.at[s, j],
                        all_recv.at[s, j],
                        dd,
                        q,
                    ).start()

                everyone(first, visit)

            owned(j, p, work)

    def wait_pile(s):
        many = 3 if s < STEPS - 1 else 1
        for j in range(slots):
            not_mine(j, many, lambda number: all_wait(s, j, number).wait_recv())

    def drain_pile(s):
        many = 3 if s < STEPS - 1 else 1
        for j in range(slots):
            not_mine(j, 3, lambda number: parts_wait(s, j, number).wait_send())
            if s == 0:
                not_mine(j, 1, lambda number: numbers_wait(j, number).wait_send())
            owned(j, p, lambda: all_wait(s, j, many * plan_count - 1).wait_send())

    lane = lax.broadcasted_iota(jnp.int32, (cx, cy), 1)
    lane_p = lax.broadcasted_iota(jnp.int32, (cz, cy), 1)

    def new_velocity(s):
        def body(z, unused):
            for c in (1, 3, 5):
                sig[c, z + 1, 7:8, :] = sigp[0, c, pl.ds(z, 1), :]
                sig[c, z + 1, cx + 8 : cx + 9, :] = sigp[1, c, pl.ds(z, 1), :]
            for c in range(3):
                i, j, k = SYM[c]
                force = sig[i, z + 2, own, :] - sig[i, z, own, :]
                force += sig[j, z + 1, pl.ds(9, cx), :] - sig[j, z + 1, pl.ds(7, cx), :]
                force += along_y(sig[k, z + 1, own, :], lane, cy)
                old = v0[c, z] if s == 0 else vx[s - 1, c, z + 2, own, :]
                at = pl.ds(pl.multiple_of(z * cx, 16), cx)
                spot = pl.ds(pl.multiple_of(c * rows + z * cx, 16), cx)
                push = acc_c[spot, :] - count_c[at, :] * old
                new = old + scale[z] * (0.5 * force + push)
                vx[s, c, z + 2, own, :] = new
                if s < STEPS - 1:
                    high, low = split_two(new)
                    thi[spot, :] = high
                    tlo[spot, :] = low
                row = pl.ds(z, 1)
                pbuf[s, 0, c, 0, row, :] = new[0:1]
                pbuf[s, 1, c, 1, row, :] = new[cx - 1 : cx]
                if s < STEPS - 1:
                    pbuf[s, 0, c, 1, row, :] = new[1:2]
                    pbuf[s, 1, c, 0, row, :] = new[cx - 2 : cx - 1]
            return unused

        lax.fori_loop(0, cz, body, 0)
        if s < STEPS - 1:
            for i in range(4):
                z = cz - 1 if i // 2 else 0
                x = cx - 1 if i % 2 else 0
                for c in range(3):
                    cbuf[s, i, c : c + 1, :] = vx[s, c, z + 2, 8 + x : 9 + x, :]

    def halo_leg(s):
        w = 2 if s < STEPS - 1 else 1
        xs0 = pl.ds(0, w)
        xs1 = pl.ds(2 - w, w)
        mid = pl.ds(8, cz)
        send = lambda i: (halo_send.at[s, i], halo_recv.at[s, i])
        copies = [
            remote(
                vx.at[s, :, pl.ds(cz + 2 - w, w), own, :],
                vx.at[s, :, pl.ds(2 - w, w), own, :],
                *send(0),
                d_up,
                p,
            ),
            remote(
                vx.at[s, :, pl.ds(2, w), own, :],
                vx.at[s, :, pl.ds(cz + 2, w), own, :],
                *send(1),
                d_dn,
                p,
            ),
            remote(pbuf.at[s, 0, :, xs0], rxp.at[s, 1, :, xs0, mid, :], *send(2), d, p_dn),
            remote(pbuf.at[s, 1, :, xs1], rxp.at[s, 0, :, xs1, mid, :], *send(3), d, p_up),
        ]
        if s < STEPS - 1:
            for i in range(4):
                copies.append(remote(cbuf.at[s, i], crx.at[s, i], *send(4 + i), *corners[i]))
        return copies

    def new_stress(s):
        last = s == STEPS - 1

        @pl.when(d == 0)
        def _():
            vx[s, :, 0:2, own, :] = jnp.zeros((3, 2, cx, cy), F32)
            if not last:
                crx[s, 2:4] = jnp.zeros((2, 3, cy), F32)

        @pl.when(d == depth_count - 1)
        def _():
            vx[s, :, cz + 2 : cz + 4, own, :] = jnp.zeros((3, 2, cx, cy), F32)
            if not last:
                crx[s, 0:2] = jnp.zeros((2, 3, cy), F32)

        @pl.when(p == 0)
        def _():
            rxp[s, 0, :, :, 8 : 8 + cz, :] = jnp.zeros((3, 2, cz, cy), F32)
            if not last:
                for i in (1, 3):
                    crx[s, i] = jnp.zeros((3, cy), F32)

        @pl.when(p == plan_count - 1)
        def _():
            rxp[s, 1, :, :, 8 : 8 + cz, :] = jnp.zeros((3, 2, cz, cy), F32)
            if not last:
                for i in (0, 2):
                    crx[s, i] = jnp.zeros((3, cy), F32)

        if not last:
            for c in range(3):
                for side in range(2):
                    x = 7 if side == 0 else cx + 8
                    below = crx[s, 3 - side, c : c + 1, :]
                    above = crx[s, 1 - side, c : c + 1, :]
                    vx[s, c, 1, x : x + 1, :] = below
                    vx[s, c, cz + 2, x : x + 1, :] = above
                    rxp[s, side, c, 1 - side, 7:8, :] = below
                    rxp[s, side, c, 1 - side, cz + 8 : cz + 9, :] = above

        def rows_in(z, unused):
            for c in range(3):
                vx[s, c, z + 2, 7:8, :] = rxp[s, 0, c, 1, pl.ds(z + 8, 1), :]
                vx[s, c, z + 2, cx + 8 : cx + 9, :] = rxp[s, 1, c, 0, pl.ds(z + 8, 1), :]
            return unused

        lax.fori_loop(0, cz, rows_in, 0)

        def body(layer, unused):
            dz = [
                vx[s, c, layer + 2, own, :] - vx[s, c, layer, own, :] for c in range(3)
            ]
            dx = [
                vx[s, c, layer + 1, pl.ds(9, cx), :] - vx[s, c, layer + 1, pl.ds(7, cx), :]
                for c in range(3)
            ]
            dy = [along_y(vx[s, c, layer + 1, own, :], lane, cy) for c in range(3)]
            flag = flg[layer]
            new = updated_stress(
                [sig[c, layer, own, :] for c in range(6)], dz, dx, dy, flag == 0, flag == 1
            )
            for c in range(6):
                sig[c, layer, own, :] = new[c]
            return unused

        if last:
            lax.fori_loop(1, cz + 1, body, 0)
            return
        lax.fori_loop(0, cz + 2, body, 0)
        for side in range(2):
            inner = [pbuf[s, side, c, side] for c in range(3)]
            outer = [rxp[s, side, c, side, 8 : 8 + cz, :] for c in range(3)]
            sign = 1.0 if side == 0 else -1.0
            ring = 1 - side
            dz = [
                rxp[s, side, c, ring, 9 : 9 + cz, :] - rxp[s, side, c, ring, 7 : 7 + cz, :]
                for c in range(3)
            ]
            dx = [sign * (inner[c] - outer[c]) for c in range(3)]
            dy = [along_y(rxp[s, side, c, ring, 8 : 8 + cz, :], lane_p, cy) for c in range(3)]
            flag = sigp[side, 6]
            new = updated_stress(
                [sigp[side, c] for c in range(6)], dz, dx, dy, flag == 0.0, flag == 1.0
            )
            for c in range(6):
                sigp[side, c] = new[c]
        clear_outside()

    def clear_outside():
        @pl.when(d == 0)
        def _():
            sig[:, 0, own, :] = jnp.zeros((6, cx, cy), F32)

        @pl.when(d == depth_count - 1)
        def _():
            sig[:, cz + 1, own, :] = jnp.zeros((6, cx, cy), F32)

        @pl.when(p == 0)
        def _():
            sigp[0, 0:6] = jnp.zeros((6, cz, cy), F32)

        @pl.when(p == plan_count - 1)
        def _():
            sigp[1, 0:6] = jnp.zeros((6, cz, cy), F32)

    def start(copies):
        for copy in copies:
            copy.start()
        return copies

    def arrive(copies):
        for copy in copies:
            copy.wait_recv()

    pile_terms(0)
    start_parts(0)
    arrive(init[0:2])
    start_numbers()
    arrive(init[2:4])
    cell_terms(0)
    arrive(init[4:])
    clear_outside()
    new_velocity(0)
    halos = [start(halo_leg(0))]
    pile_terms(1)
    start_parts(1)
    update_pile(0)
    arrive(halos[0])
    new_stress(0)
    wait_pile(0)
    cell_terms(1)
    update_pile(1)
    new_velocity(1)
    halos.append(start(halo_leg(1)))
    pile_terms(2)
    start_parts(2)
    arrive(halos[1])
    new_stress(1)
    wait_pile(1)
    cell_terms(2)
    new_velocity(2)
    halos.append(start(halo_leg(2)))
    velocity_back = pltpu.make_async_copy(
        vx.at[2, :, pl.ds(2, cz), own, :], velocity_out, local_sem.at[0]
    )
    velocity_back.start()
    update_pile(2)
    arrive(halos[2])
    new_stress(2)
    stress_back = pltpu.make_async_copy(
        sig.at[:, pl.ds(1, cz), own, :], stress_out, local_sem.at[1]
    )
    stress_back.start()
    wait_pile(2)

    def pile_lines(t, unused):
        for r in range(8):
            at = pl.ds(pl.multiple_of(t * 1024 + r * 128, 128), 128)
            for c in range(3):
                pilev[c : c + 1, at] = pvw[STEPS, units + c * tiles + t, r : r + 1, :]
        return unused

    lax.fori_loop(0, tiles, pile_lines, 0)
    pile_back = pltpu.make_async_copy(pilev, pile_out, local_sem.at[2])
    pile_back.start()

    for copies in [init] + halos:
        for copy in copies:
            copy.wait_send()
    for s in range(STEPS):
        drain_pile(s)
    velocity_back.wait()
    stress_back.wait()
    pile_back.wait()


def shards(
    depth_count,
    plan_count,
    stress,
    velocity,
    density,
    flags,
    pile_velocity,
    pile_mass,
    jack_force,
    pair_elem,
    pair_cell,
):
    cz, cx, cy = density.shape
    width = pile_mass.shape[0]
    tiles = width // 1024
    pairs = pair_elem.shape[1]
    chunk = min(512, pairs)
    units = 3 * tiles
    slots = -(-units // plan_count)
    rows = cz * cx
    prows = -(-(3 * width // 256) // 16) * 16
    sizes = (depth_count, plan_count, cz, cx, cy, tiles, pairs, chunk)
    vm = lambda *shape: pltpu.VMEM(shape, F32)
    half = lambda *shape: pltpu.VMEM(shape, BF16)
    whole = lambda *shape: pltpu.VMEM(shape, jnp.int32)
    dma = lambda *shape: pltpu.SemaphoreType.DMA(shape)
    scratch = [
        vm(6, cz + 2, cx + 16, cy),
        vm(STEPS, 3, cz + 4, cx + 16, cy),
        vm(3, cz, cx, cy),
        vm(cz, cx, cy),
        whole(cz + 2, cx, cy),
        vm(2, 7, cz, cy),
        vm(2, 7, cz, cy),
        vm(STEPS, 2, 3, 2, cz, cy),
        vm(STEPS, 2, 3, 2, cz + 16, cy),
        vm(STEPS, 4, 3, cy),
        vm(STEPS, 4, 3, cy),
        vm(STEPS + 1, 3 * units, 8, 128),
        vm(tiles, 8, 128),
        vm(units, 8, 128),
        vm(3, width),
        vm(3, width),
        whole(1, pairs),
        whole(1, pairs),
        whole(1, pairs),
        whole(1, pairs),
        half(cy, pairs),
        half(rows, pairs),
        half(256, pairs),
        half(prows, pairs),
        half(3 * rows, cy),
        half(3 * rows, cy),
        vm(3 * prows, 256),
        half(2, 3 * prows, 256),
        vm(3 * prows, 256),
        vm(3 * rows, cy),
        vm(rows, cy),
        vm(STEPS, 3, units, 8, 128),
        vm(STEPS, slots, 3 * plan_count, 8, 128),
        vm(3, tiles, 8, 128),
        vm(2, tiles, 8, 128),
        vm(tiles, 8, 128),
        vm(slots, plan_count, 8, 128),
        vm(slots, 8, 128),
        dma(9),
        dma(8),
        dma(8),
        dma(STEPS, 8),
        dma(STEPS, 8),
        dma(2),
        dma(2),
        dma(STEPS, slots),
        dma(STEPS, slots),
        dma(slots),
        dma(slots),
        dma(STEPS, slots),
        dma(STEPS, slots),
    ]
    anywhere = pl.BlockSpec(memory_space=pl.ANY)
    stress, velocity, pile = pl.pallas_call(
        functools.partial(kernel, sizes),
        out_shape=(
            jax.ShapeDtypeStruct(stress.shape, F32),
            jax.ShapeDtypeStruct(velocity.shape, F32),
            jax.ShapeDtypeStruct((3, width), F32),
        ),
        in_specs=[anywhere] * 9,
        out_specs=(anywhere,) * 3,
        scratch_shapes=scratch,
        compiler_params=pltpu.CompilerParams(
            collective_id=0, has_side_effects=True, vmem_limit_bytes=60 * 1024 * 1024
        ),
    )(
        stress,
        velocity,
        density,
        flags,
        pile_velocity,
        pile_mass.reshape(tiles, 8, 128),
        jack_force,
        pair_elem,
        pair_cell,
    )
    return stress, velocity, pile


def solution(mesh):
    field = P(None, "depth", "plan", None)
    cells = P("depth", "plan", None)
    placed = (
        field,
        field,
        cells,
        cells,
        P(None, "depth"),
        P("depth"),
        P(None, "depth"),
        P("depth", "plan"),
        P("depth", "plan"),
    )
    return jax.shard_map(
        functools.partial(shards, mesh.shape["depth"], mesh.shape["plan"]),
        mesh=mesh,
        in_specs=placed,
        out_specs=(field, field, P(None, "depth")),
        check_vma=False,
    )
```

```python
import functools

import jax
import jax.numpy as jnp
from jax import lax
from jax.experimental import pallas as pl
from jax.experimental.pallas import tpu as pltpu
from jax.sharding import PartitionSpec as P

STEPS = 3
DT = 0.2
MESH = pl.DeviceIdType.MESH
F32 = jnp.float32
BF16 = jnp.bfloat16
SYM = ((0, 3, 4), (3, 1, 5), (4, 5, 2))
SUMS_IN_TWO = (0, 1, 2)
TILES_IN_TWO = (0, 1)


def split_two(x):
    high = x.astype(BF16)
    return high, (x - high.astype(F32)).astype(BF16)


def dot_nn(a, b):
    return jnp.dot(a, b, preferred_element_type=F32)


def dot_nt(a, b):
    return lax.dot_general(a, b, (((1,), (1,)), ((), ())), preferred_element_type=F32)


def along_y(a, lane, width):
    after = jnp.where(lane < width - 1, pltpu.roll(a, width - 1, 1), 0.0)
    before = jnp.where(lane > 0, pltpu.roll(a, 1, 1), 0.0)
    return after - before


def updated_stress(sig, dz, dx, dy, elastic, cone):
    half = 0.5 * DT
    common = half * (dz[0] + dx[1] + dy[2])
    trial = [
        sig[0] + DT * dz[0] + common,
        sig[1] + DT * dx[1] + common,
        sig[2] + DT * dy[2] + common,
        sig[3] + half * (dx[0] + dz[1]),
        sig[4] + half * (dy[0] + dz[2]),
        sig[5] + half * (dy[1] + dx[2]),
    ]
    pressure = (trial[0] + trial[1] + trial[2]) * (1.0 / 3.0)
    dev = [trial[i] - pressure for i in range(3)]
    second = 0.5 * (dev[0] * dev[0] + dev[1] * dev[1] + dev[2] * dev[2]) + (
        trial[3] * trial[3] + trial[4] * trial[4] + trial[5] * trial[5]
    )
    shrink = 1.0 / (1.0 + 1.5 * jnp.sqrt(second))
    factor = jnp.where(elastic, 1.0, jnp.where(cone, shrink, 0.0))
    new = [dev[i] * factor + pressure for i in range(3)]
    return new + [trial[i] * factor for i in range(3, 6)]


def kernel(
    sizes,
    stress,
    velocity,
    density,
    flags,
    pile0,
    mass,
    jack,
    pair_elem,
    pair_cell,
    stress_out,
    velocity_out,
    pile_out,
    sig,
    vx,
    v0,
    scale,
    flg,
    sigp,
    spk,
    pbuf,
    rxp,
    cbuf,
    crx,
    pvw,
    massv,
    jackv,
    pilev,
    jackw,
    elemv,
    cellv,
    crow,
    prow,
    acol,
    arow,
    bcol,
    brow,
    thi,
    tlo,
    phi,
    plo,
    acc_s,
    acc_c,
    count_c,
    sbuf,
    sdep,
    sown,
    rx,
    nbuf,
    ndep,
    nsum,
    rxn,
    nown,
    local_sem,
    init_send,
    init_recv,
    halo_send,
    halo_recv,
    dep_send,
    dep_recv,
    part_send,
    part_recv,
    num_send,
    num_recv,
    all_send,
    all_recv,
    leg_send,
    leg_recv,
    win_send,
    win_recv,
):
    depth_count, plan_count, cz, cx, cy, tiles, pairs, chunk = sizes
    units = 3 * tiles
    slots = -(-units // plan_count)
    rows = cz * cx
    prows = brow.shape[0]
    block_rows = tiles // 2 * 8
    d = lax.axis_index("depth")
    p = lax.axis_index("plan")
    d_up = lax.rem(d + 1, depth_count)
    d_dn = lax.rem(d + depth_count - 1, depth_count)
    p_up = lax.rem(p + 1, plan_count)
    p_dn = lax.rem(p + plan_count - 1, plan_count)
    own = pl.ds(8, cx)
    y_count = plan_count // 2
    y = p // 2
    z_low = p % 2
    odd = d % 2
    d_near = d + 1 - 2 * odd
    d_far = lax.rem(d + depth_count - 1 + 2 * odd, depth_count)
    kinds = ((d_far, 2 * odd), (d_near, 2 - 2 * odd), (d, 1))

    def everyone(first, visit):
        def body(i, unused):
            step = (i + 1) // 2
            yy = lax.rem(y + y_count // 2 + step * (1 - 2 * (i % 2)) + y_count, y_count)
            for kind in range(first, 3):
                dd, block = kinds[kind]
                for z in (1 - z_low, z_low):
                    act = functools.partial(visit, kind, dd, block, yy * 2 + z)
                    if kind == 2 and z is z_low:
                        pl.when(i < y_count - 1)(act)
                    else:
                        act()
            return unused

        lax.fori_loop(0, y_count, body, 0)

    def remote(src, dst, send, recv, dd, pp):
        return pltpu.make_async_remote_copy(
            src_ref=src,
            dst_ref=dst,
            send_sem=send,
            recv_sem=recv,
            device_id={"depth": dd, "plan": pp},
            device_id_type=MESH,
        )

    local = [
        (stress, sig.at[:, pl.ds(1, cz), own, :]),
        (velocity, v0),
        (density, scale),
        (flags, flg.at[pl.ds(1, cz)]),
        (pile0, pilev),
        (mass, massv),
        (jack, jackw),
        (pair_elem, elemv),
        (pair_cell, cellv),
    ]
    local = [
        pltpu.make_async_copy(src, dst, local_sem.at[i]) for i, (src, dst) in enumerate(local)
    ]
    for copy in local:
        copy.start()

    barrier = pltpu.get_barrier_semaphore()
    corners = ((d_dn, p_dn), (d_dn, p_up), (d_up, p_dn), (d_up, p_up))

    def greet(kind, dd, block, q):
        pl.semaphore_signal(
            barrier, inc=1, device_id={"depth": dd, "plan": q}, device_id_type=MESH
        )

    everyone(0, greet)
    for i in (0, 3):
        local[i].wait()

    def pack_edges(z, unused):
        at = pl.ds(z, 1)
        for c in range(6):
            spk[0, c, at, :] = sig[c, z + 1, 8:9, :]
            spk[1, c, at, :] = sig[c, z + 1, cx + 7 : cx + 8, :]
        spk[0, 6, at, :] = flg[z + 1, 0:1, :].astype(F32)
        spk[1, 6, at, :] = flg[z + 1, cx - 1 : cx, :].astype(F32)
        return unused

    lax.fori_loop(0, cz, pack_edges, 0)

    local[4].wait()
    local[6].wait()

    def pile_tiles(t, unused):
        for r in range(8):
            at = pl.ds(pl.multiple_of(t * 1024 + r * 128, 128), 128)
            for source, target, first in ((pilev, pvw.at[0], units), (jackw, jackv, 0)):
                value = source[:, at]
                for c in range(3):
                    target[first + c * tiles + t, r : r + 1, :] = value[c : c + 1]
        return unused

    lax.fori_loop(0, tiles, pile_tiles, 0)
    for i in (1, 2, 5, 7, 8):
        local[i].wait()

    def tables(i, unused):
        at = pl.ds(pl.multiple_of(i * chunk, chunk), chunk)
        cell = cellv[:, at]
        elem = elemv[:, at]
        live = cell >= 0
        c_row = jnp.where(live, cell // cy, -1)
        c_col = jnp.where(live, cell % cy, -1)
        block = elem // (tiles * 1024)
        inner = elem - block * (tiles * 1024)
        half_row = inner // 128
        p_row = block * block_rows + (half_row // 16) * 8 + half_row % 8
        p_col = (half_row // 8 % 2) * 128 + inner % 128
        p_row = jnp.where(live, p_row, -1)
        crow[:, at] = c_row
        prow[:, at] = p_row
        across = lax.broadcasted_iota(jnp.int32, (cy, chunk), 0)
        acol[:, at] = (across == c_col).astype(F32).astype(BF16)
        arow[:, at] = (across[:rows] == c_row).astype(F32).astype(BF16)
        wide = lax.broadcasted_iota(jnp.int32, (256, chunk), 0)
        bcol[:, at] = (wide == p_col).astype(F32).astype(BF16)
        brow[:, at] = (wide[:prows] == p_row).astype(F32).astype(BF16)
        return unused

    lax.fori_loop(0, pairs // chunk, tables, 0)

    def split_start(z, unused):
        for c in range(3):
            high, low = split_two(v0[c, z])
            at = pl.ds(pl.multiple_of(c * rows + z * cx, 16), cx)
            thi[at, :] = high
            tlo[at, :] = low
        scale[z] = DT / scale[z]
        return unused

    lax.fori_loop(0, cz, split_start, 0)
    def pile_terms(s):
        acc_s[...] = jnp.zeros_like(acc_s)

        def body(i, unused):
            at = pl.ds(pl.multiple_of(i * chunk, chunk), chunk)
            col = acol[:, at]
            picked = dot_nn(thi[...], col) + dot_nn(tlo[...], col)
            here = lax.broadcasted_iota(jnp.int32, (rows, chunk), 0) == crow[:, at]
            row = brow[:, at]
            high, low = [], []
            for c in range(3):
                value = jnp.sum(
                    jnp.where(here, picked[c * rows : (c + 1) * rows], 0.0), axis=0, keepdims=True
                )
                first, second = split_two(value)
                high.append(row * first)
                low.append(row * second)
            wide = bcol[:, at]
            acc_s[...] += dot_nt(jnp.concatenate(high, 0), wide) + dot_nt(
                jnp.concatenate(low, 0), wide
            )
            return unused

        lax.fori_loop(0, pairs // chunk, body, 0, unroll=True)
        for b in range(3):
            for c in range(3):
                for t in range(tiles):
                    r = c * prows + b * block_rows + t // 2 * 8
                    l = t % 2 * 128
                    sbuf[s, b, c * tiles + t] = acc_s[r : r + 8, l : l + 128]

    def cell_terms(s):
        for b in range(3):
            for c in range(3):
                for a in range(tiles // 2):
                    u = b * units + c * tiles + 2 * a
                    r = c * prows + b * block_rows + a * 8
                    phi[r : r + 8, 0:128] = pvw[s, u]
                    phi[r : r + 8, 128:256] = pvw[s, u + 1]
        high, low = split_two(phi[...])
        plo[0] = high
        plo[1] = low

        picked = dot_nn(plo[0], bcol[...]) + dot_nn(plo[1], bcol[...])
        here = lax.broadcasted_iota(jnp.int32, (prows, pairs), 0) == prow[...]
        high, low = [], []
        for c in range(3):
            value = jnp.sum(
                jnp.where(here, picked[c * prows : (c + 1) * prows], 0.0), axis=0, keepdims=True
            )
            first, second = split_two(value)
            high.append(arow[...] * first)
            low.append(arow[...] * second)
        acc_c[...] = dot_nt(jnp.concatenate(high, 0), acol[...]) + dot_nt(
            jnp.concatenate(low, 0), acol[...]
        )


    count_c[...] = dot_nt(arow[...], acol[...])
    acc_s[0:prows, :] = dot_nt(brow[...], bcol[...])
    for b in range(3):
        for t in range(tiles):
            r = b * block_rows + t // 2 * 8
            l = t % 2 * 128
            nbuf[b, t] = acc_s[r : r + 8, l : l + 128]
    phi[...] = jnp.zeros_like(phi)
    pile_terms(0)
    pl.semaphore_wait(barrier, 3 * plan_count - 1)
    mine = pl.ds(units, units)
    init = [
        remote(
            nbuf.at[0], ndep.at[1], dep_send.at[0], dep_recv.at[0], d_dn, p
        ),
        remote(
            nbuf.at[2], ndep.at[0], dep_send.at[1], dep_recv.at[1], d_up, p
        ),
        remote(
            pvw.at[0, mine],
            pvw.at[0, pl.ds(0, units)],
            init_send.at[0],
            init_recv.at[0],
            d_up,
            p,
        ),
        remote(
            pvw.at[0, mine],
            pvw.at[0, pl.ds(2 * units, units)],
            init_send.at[1],
            init_recv.at[1],
            d_dn,
            p,
        ),
        remote(
            stress.at[:, cz - 1], sig.at[:, 0, own, :], init_send.at[2], init_recv.at[2], d_up, p
        ),
        remote(
            stress.at[:, 0], sig.at[:, cz + 1, own, :], init_send.at[3], init_recv.at[3], d_dn, p
        ),
        remote(spk.at[0], sigp.at[1], init_send.at[4], init_recv.at[4], d, p_dn),
        remote(spk.at[1], sigp.at[0], init_send.at[5], init_recv.at[5], d, p_up),
        remote(flags.at[cz - 1], flg.at[0], init_send.at[6], init_recv.at[6], d_up, p),
        remote(flags.at[0], flg.at[cz + 1], init_send.at[7], init_recv.at[7], d_dn, p),
    ]

    def depth_leg(s):
        return [
            remote(sbuf.at[s, 0], sdep.at[s, 1], leg_send.at[s, 0], leg_recv.at[s, 0], d_dn, p),
            remote(sbuf.at[s, 2], sdep.at[s, 0], leg_send.at[s, 1], leg_recv.at[s, 1], d_up, p),
        ]

    def window_leg(s):
        block = lambda b: pvw.at[s + 1, pl.ds(b * units, units)]
        return [
            remote(block(1), block(0), win_send.at[s, 0], win_recv.at[s, 0], d_up, p),
            remote(block(1), block(2), win_send.at[s, 1], win_recv.at[s, 1], d_dn, p),
        ]

    def owned(j, q, work):
        if plan_count * (j + 1) <= units:
            work()
        else:
            pl.when(q + plan_count * j < units)(work)

    def send_parts(s):
        def visit(kind, dd, block, q):
            for j in range(slots):
                u = q + plan_count * j
                source = sown.at[s, u] if s in SUMS_IN_TWO else sbuf.at[s, block, u]
                owned(
                    j,
                    q,
                    lambda: remote(
                        source,
                        rx.at[s, j, kind * plan_count + p],
                        part_send.at[s, j],
                        part_recv.at[s, j],
                        dd,
                        q,
                    ).start(),
                )

        everyone(2 if s in SUMS_IN_TWO else 0, visit)

    def start_parts(s):
        if s in SUMS_IN_TWO:
            for copy in depth_leg(s):
                copy.start()
        else:
            send_parts(s)

    def middle_parts(s):
        if s in SUMS_IN_TWO:
            for copy in depth_leg(s):
                copy.wait_recv()
            for u in range(units):
                sown[s, u] = sbuf[s, 1, u] + sdep[s, 0, u] + sdep[s, 1, u]
            send_parts(s)

    def start_numbers():
        for t in range(tiles):
            nsum[t] = nbuf[1, t] + ndep[0, t] + ndep[1, t]

        def visit(kind, dd, block, q):
            for j in range(slots):
                owned(
                    j,
                    q,
                    lambda: remote(
                        nsum.at[lax.rem(q + plan_count * j, tiles)],
                        rxn.at[j, p],
                        num_send.at[j],
                        num_recv.at[j],
                        d,
                        q,
                    ).start(),
                )

        everyone(2, visit)

    def some_of(ref, number, send, recv):
        some = ref.at[pl.ds(0, number)]
        return remote(some, some, send, recv, d, p_up)

    def parts_wait(s, j, number):
        return some_of(rx.at[s, j], number, part_send.at[s, j], part_recv.at[s, j])

    def numbers_wait(j, number):
        return some_of(rxn.at[j], number, num_send.at[j], num_recv.at[j])

    def all_wait(s, j, number):
        return some_of(pvw.at[s + 1], number, all_send.at[s, j], all_recv.at[s, j])

    def not_mine(j, many, act):
        here = min(plan_count, units - plan_count * j)
        if here == plan_count:
            act(here * many - 1)
        else:
            if here * many > 1:
                pl.when(p < here)(lambda: act(here * many - 1))
            pl.when(p >= here)(lambda: act(here * many))

    def update_pile(s):
        first = 2 if s in TILES_IN_TWO or s == STEPS - 1 else 0
        two = s in SUMS_IN_TWO
        for j in range(slots):
            u = p + plan_count * j

            def work():
                t = lax.rem(u, tiles)
                parts_wait(s, j, (1 if two else 3) * plan_count - 1).wait_recv()
                rx[s, j, 2 * plan_count + p] = sown[s, u] if two else sbuf[s, 1, u]
                if s == 0:
                    numbers_wait(j, plan_count - 1).wait_recv()
                    rxn[j, p] = nsum[t]
                    nown[j] = jnp.sum(rxn[j], axis=0)
                before = pvw[s, units + u]
                force = jackv[u] + jnp.sum(rx[s, j, (2 * plan_count if two else 0) :], axis=0) - nown[j] * before
                pvw[s + 1, units + u] = before + DT * force / massv[t]

                def visit(kind, dd, block, q):
                    remote(
                        pvw.at[s + 1, units + u],
                        pvw.at[s + 1, (2 - block) * units + u],
                        all_send.at[s, j],
                        all_recv.at[s, j],
                        dd,
                        q,
                    ).start()

                everyone(first, visit)

            owned(j, p, work)

    def own_pile(s):
        if s in TILES_IN_TWO:
            for j in range(slots):
                not_mine(j, 1, lambda number: all_wait(s, j, number).wait_recv())
            for copy in window_leg(s):
                copy.start()

    def wait_pile(s):
        if s in TILES_IN_TWO:
            for copy in window_leg(s):
                copy.wait_recv()
            return
        many = 3 if s < STEPS - 1 else 1
        for j in range(slots):
            not_mine(j, many, lambda number: all_wait(s, j, number).wait_recv())

    def drain_pile(s):
        many = 1 if s in TILES_IN_TWO or s == STEPS - 1 else 3
        sums = 1 if s in SUMS_IN_TWO else 3
        if s in SUMS_IN_TWO:
            for copy in depth_leg(s):
                copy.wait_send()
        if s in TILES_IN_TWO:
            for copy in window_leg(s):
                copy.wait_send()
        for j in range(slots):
            not_mine(j, sums, lambda number: parts_wait(s, j, number).wait_send())
            if s == 0:
                not_mine(j, 1, lambda number: numbers_wait(j, number).wait_send())
            owned(j, p, lambda: all_wait(s, j, many * plan_count - 1).wait_send())

    lane = lax.broadcasted_iota(jnp.int32, (cx, cy), 1)
    lane_p = lax.broadcasted_iota(jnp.int32, (cz, cy), 1)

    def new_velocity(s):
        def body(z, unused):
            for c in (1, 3, 5):
                sig[c, z + 1, 7:8, :] = sigp[0, c, pl.ds(z, 1), :]
                sig[c, z + 1, cx + 8 : cx + 9, :] = sigp[1, c, pl.ds(z, 1), :]
            for c in range(3):
                i, j, k = SYM[c]
                force = sig[i, z + 2, own, :] - sig[i, z, own, :]
                force += sig[j, z + 1, pl.ds(9, cx), :] - sig[j, z + 1, pl.ds(7, cx), :]
                force += along_y(sig[k, z + 1, own, :], lane, cy)
                old = v0[c, z] if s == 0 else vx[s - 1, c, z + 2, own, :]
                at = pl.ds(pl.multiple_of(z * cx, 16), cx)
                spot = pl.ds(pl.multiple_of(c * rows + z * cx, 16), cx)
                push = acc_c[spot, :] - count_c[at, :] * old
                new = old + scale[z] * (0.5 * force + push)
                vx[s, c, z + 2, own, :] = new
                if s < STEPS - 1:
                    high, low = split_two(new)
                    thi[spot, :] = high
                    tlo[spot, :] = low
                row = pl.ds(z, 1)
                pbuf[s, 0, c, 0, row, :] = new[0:1]
                pbuf[s, 1, c, 1, row, :] = new[cx - 1 : cx]
                if s < STEPS - 1:
                    pbuf[s, 0, c, 1, row, :] = new[1:2]
                    pbuf[s, 1, c, 0, row, :] = new[cx - 2 : cx - 1]
            return unused

        lax.fori_loop(0, cz, body, 0)
        if s < STEPS - 1:
            for i in range(4):
                z = cz - 1 if i // 2 else 0
                x = cx - 1 if i % 2 else 0
                for c in range(3):
                    cbuf[s, i, c : c + 1, :] = vx[s, c, z + 2, 8 + x : 9 + x, :]

    def halo_leg(s):
        w = 2 if s < STEPS - 1 else 1
        xs0 = pl.ds(0, w)
        xs1 = pl.ds(2 - w, w)
        mid = pl.ds(8, cz)
        send = lambda i: (halo_send.at[s, i], halo_recv.at[s, i])
        copies = [
            remote(
                vx.at[s, :, pl.ds(cz + 2 - w, w), own, :],
                vx.at[s, :, pl.ds(2 - w, w), own, :],
                *send(0),
                d_up,
                p,
            ),
            remote(
                vx.at[s, :, pl.ds(2, w), own, :],
                vx.at[s, :, pl.ds(cz + 2, w), own, :],
                *send(1),
                d_dn,
                p,
            ),
            remote(pbuf.at[s, 0, :, xs0], rxp.at[s, 1, :, xs0, mid, :], *send(2), d, p_dn),
            remote(pbuf.at[s, 1, :, xs1], rxp.at[s, 0, :, xs1, mid, :], *send(3), d, p_up),
        ]
        if s < STEPS - 1:
            for i in range(4):
                copies.append(remote(cbuf.at[s, i], crx.at[s, i], *send(4 + i), *corners[i]))
        return copies

    def new_stress(s):
        last = s == STEPS - 1

        @pl.when(d == 0)
        def _():
            vx[s, :, 0:2, own, :] = jnp.zeros((3, 2, cx, cy), F32)
            if not last:
                crx[s, 2:4] = jnp.zeros((2, 3, cy), F32)

        @pl.when(d == depth_count - 1)
        def _():
            vx[s, :, cz + 2 : cz + 4, own, :] = jnp.zeros((3, 2, cx, cy), F32)
            if not last:
                crx[s, 0:2] = jnp.zeros((2, 3, cy), F32)

        @pl.when(p == 0)
        def _():
            rxp[s, 0, :, :, 8 : 8 + cz, :] = jnp.zeros((3, 2, cz, cy), F32)
            if not last:
                for i in (1, 3):
                    crx[s, i] = jnp.zeros((3, cy), F32)

        @pl.when(p == plan_count - 1)
        def _():
            rxp[s, 1, :, :, 8 : 8 + cz, :] = jnp.zeros((3, 2, cz, cy), F32)
            if not last:
                for i in (0, 2):
                    crx[s, i] = jnp.zeros((3, cy), F32)

        if not last:
            for c in range(3):
                for side in range(2):
                    x = 7 if side == 0 else cx + 8
                    below = crx[s, 3 - side, c : c + 1, :]
                    above = crx[s, 1 - side, c : c + 1, :]
                    vx[s, c, 1, x : x + 1, :] = below
                    vx[s, c, cz + 2, x : x + 1, :] = above
                    rxp[s, side, c, 1 - side, 7:8, :] = below
                    rxp[s, side, c, 1 - side, cz + 8 : cz + 9, :] = above

        def rows_in(z, unused):
            for c in range(3):
                vx[s, c, z + 2, 7:8, :] = rxp[s, 0, c, 1, pl.ds(z + 8, 1), :]
                vx[s, c, z + 2, cx + 8 : cx + 9, :] = rxp[s, 1, c, 0, pl.ds(z + 8, 1), :]
            return unused

        lax.fori_loop(0, cz, rows_in, 0)

        def body(layer, unused):
            dz = [
                vx[s, c, layer + 2, own, :] - vx[s, c, layer, own, :] for c in range(3)
            ]
            dx = [
                vx[s, c, layer + 1, pl.ds(9, cx), :] - vx[s, c, layer + 1, pl.ds(7, cx), :]
                for c in range(3)
            ]
            dy = [along_y(vx[s, c, layer + 1, own, :], lane, cy) for c in range(3)]
            flag = flg[layer]
            new = updated_stress(
                [sig[c, layer, own, :] for c in range(6)], dz, dx, dy, flag == 0, flag == 1
            )
            for c in range(6):
                sig[c, layer, own, :] = new[c]
            return unused

        if last:
            lax.fori_loop(1, cz + 1, body, 0)
            return
        lax.fori_loop(0, cz + 2, body, 0)
        for side in range(2):
            inner = [pbuf[s, side, c, side] for c in range(3)]
            outer = [rxp[s, side, c, side, 8 : 8 + cz, :] for c in range(3)]
            sign = 1.0 if side == 0 else -1.0
            ring = 1 - side
            dz = [
                rxp[s, side, c, ring, 9 : 9 + cz, :] - rxp[s, side, c, ring, 7 : 7 + cz, :]
                for c in range(3)
            ]
            dx = [sign * (inner[c] - outer[c]) for c in range(3)]
            dy = [along_y(rxp[s, side, c, ring, 8 : 8 + cz, :], lane_p, cy) for c in range(3)]
            flag = sigp[side, 6]
            new = updated_stress(
                [sigp[side, c] for c in range(6)], dz, dx, dy, flag == 0.0, flag == 1.0
            )
            for c in range(6):
                sigp[side, c] = new[c]
        clear_outside()

    def clear_outside():
        @pl.when(d == 0)
        def _():
            sig[:, 0, own, :] = jnp.zeros((6, cx, cy), F32)

        @pl.when(d == depth_count - 1)
        def _():
            sig[:, cz + 1, own, :] = jnp.zeros((6, cx, cy), F32)

        @pl.when(p == 0)
        def _():
            sigp[0, 0:6] = jnp.zeros((6, cz, cy), F32)

        @pl.when(p == plan_count - 1)
        def _():
            sigp[1, 0:6] = jnp.zeros((6, cz, cy), F32)

    def start(copies):
        for copy in copies:
            copy.start()
        return copies

    def arrive(copies):
        for copy in copies:
            copy.wait_recv()

    start(init[0:2])
    start_parts(0)
    start(init[2:])
    arrive(init[0:2])
    start_numbers()
    middle_parts(0)
    arrive(init[2:4])
    cell_terms(0)
    arrive(init[4:])
    clear_outside()
    new_velocity(0)
    halos = [start(halo_leg(0))]
    pile_terms(1)
    start_parts(1)
    update_pile(0)
    middle_parts(1)
    own_pile(0)
    arrive(halos[0])
    new_stress(0)
    update_pile(1)
    wait_pile(0)
    cell_terms(1)
    new_velocity(1)
    halos.append(start(halo_leg(1)))
    pile_terms(2)
    start_parts(2)
    own_pile(1)
    middle_parts(2)
    arrive(halos[1])
    new_stress(1)
    wait_pile(1)
    cell_terms(2)
    new_velocity(2)
    halos.append(start(halo_leg(2)))
    velocity_back = pltpu.make_async_copy(
        vx.at[2, :, pl.ds(2, cz), own, :], velocity_out, local_sem.at[0]
    )
    velocity_back.start()
    update_pile(2)
    arrive(halos[2])
    new_stress(2)
    stress_back = pltpu.make_async_copy(
        sig.at[:, pl.ds(1, cz), own, :], stress_out, local_sem.at[1]
    )
    stress_back.start()
    wait_pile(2)

    def pile_lines(t, unused):
        for r in range(8):
            at = pl.ds(pl.multiple_of(t * 1024 + r * 128, 128), 128)
            for c in range(3):
                pilev[c : c + 1, at] = pvw[STEPS, units + c * tiles + t, r : r + 1, :]
        return unused

    lax.fori_loop(0, tiles, pile_lines, 0)
    pile_back = pltpu.make_async_copy(pilev, pile_out, local_sem.at[2])
    pile_back.start()

    for copies in [init] + halos:
        for copy in copies:
            copy.wait_send()
    for s in range(STEPS):
        drain_pile(s)
    velocity_back.wait()
    stress_back.wait()
    pile_back.wait()


def shards(
    depth_count,
    plan_count,
    stress,
    velocity,
    density,
    flags,
    pile_velocity,
    pile_mass,
    jack_force,
    pair_elem,
    pair_cell,
):
    cz, cx, cy = density.shape
    width = pile_mass.shape[0]
    tiles = width // 1024
    pairs = pair_elem.shape[1]
    chunk = min(1024, pairs)
    units = 3 * tiles
    slots = -(-units // plan_count)
    rows = cz * cx
    prows = -(-(3 * width // 256) // 16) * 16
    sizes = (depth_count, plan_count, cz, cx, cy, tiles, pairs, chunk)
    vm = lambda *shape: pltpu.VMEM(shape, F32)
    half = lambda *shape: pltpu.VMEM(shape, BF16)
    whole = lambda *shape: pltpu.VMEM(shape, jnp.int32)
    dma = lambda *shape: pltpu.SemaphoreType.DMA(shape)
    scratch = [
        vm(6, cz + 2, cx + 16, cy),
        vm(STEPS, 3, cz + 4, cx + 16, cy),
        vm(3, cz, cx, cy),
        vm(cz, cx, cy),
        whole(cz + 2, cx, cy),
        vm(2, 7, cz, cy),
        vm(2, 7, cz, cy),
        vm(STEPS, 2, 3, 2, cz, cy),
        vm(STEPS, 2, 3, 2, cz + 16, cy),
        vm(STEPS, 4, 3, cy),
        vm(STEPS, 4, 3, cy),
        vm(STEPS + 1, 3 * units, 8, 128),
        vm(tiles, 8, 128),
        vm(units, 8, 128),
        vm(3, width),
        vm(3, width),
        whole(1, pairs),
        whole(1, pairs),
        whole(1, pairs),
        whole(1, pairs),
        half(cy, pairs),
        half(rows, pairs),
        half(256, pairs),
        half(prows, pairs),
        half(3 * rows, cy),
        half(3 * rows, cy),
        vm(3 * prows, 256),
        half(2, 3 * prows, 256),
        vm(3 * prows, 256),
        vm(3 * rows, cy),
        vm(rows, cy),
        vm(STEPS, 3, units, 8, 128),
        vm(STEPS, 2, units, 8, 128),
        vm(STEPS, units, 8, 128),
        vm(STEPS, slots, 3 * plan_count, 8, 128),
        vm(3, tiles, 8, 128),
        vm(2, tiles, 8, 128),
        vm(tiles, 8, 128),
        vm(slots, plan_count, 8, 128),
        vm(slots, 8, 128),
        dma(9),
        dma(8),
        dma(8),
        dma(STEPS, 8),
        dma(STEPS, 8),
        dma(2),
        dma(2),
        dma(STEPS, slots),
        dma(STEPS, slots),
        dma(slots),
        dma(slots),
        dma(STEPS, slots),
        dma(STEPS, slots),
        dma(STEPS, 2),
        dma(STEPS, 2),
        dma(STEPS, 2),
        dma(STEPS, 2),
    ]
    anywhere = pl.BlockSpec(memory_space=pl.ANY)
    stress, velocity, pile = pl.pallas_call(
        functools.partial(kernel, sizes),
        out_shape=(
            jax.ShapeDtypeStruct(stress.shape, F32),
            jax.ShapeDtypeStruct(velocity.shape, F32),
            jax.ShapeDtypeStruct((3, width), F32),
        ),
        in_specs=[anywhere] * 9,
        out_specs=(anywhere,) * 3,
        scratch_shapes=scratch,
        compiler_params=pltpu.CompilerParams(
            collective_id=0, has_side_effects=True, vmem_limit_bytes=60 * 1024 * 1024
        ),
    )(
        stress,
        velocity,
        density,
        flags,
        pile_velocity,
        pile_mass.reshape(tiles, 8, 128),
        jack_force,
        pair_elem,
        pair_cell,
    )
    return stress, velocity, pile


def solution(mesh):
    field = P(None, "depth", "plan", None)
    cells = P("depth", "plan", None)
    placed = (
        field,
        field,
        cells,
        cells,
        P(None, "depth"),
        P("depth"),
        P(None, "depth"),
        P("depth", "plan"),
        P("depth", "plan"),
    )
    return jax.shard_map(
        functools.partial(shards, mesh.shape["depth"], mesh.shape["plan"]),
        mesh=mesh,
        in_specs=placed,
        out_specs=(field, field, P(None, "depth")),
        check_vma=False,
    )
```

```python
import functools

import jax
import jax.numpy as jnp
from jax import lax
from jax.experimental import pallas as pl
from jax.experimental.pallas import tpu as pltpu
from jax.sharding import PartitionSpec as P

STEPS = 3
DT = 0.2
MESH = pl.DeviceIdType.MESH
F32 = jnp.float32
BF16 = jnp.bfloat16
SYM = ((0, 3, 4), (3, 1, 5), (4, 5, 2))
SUMS_IN_TWO = (0, 1, 2)
TILES_IN_TWO = (0, 1)


def split_two(x):
    high = x.astype(BF16)
    return high, (x - high.astype(F32)).astype(BF16)


def dot_nn(a, b):
    return jnp.dot(a, b, preferred_element_type=F32)


def dot_nt(a, b):
    return lax.dot_general(a, b, (((1,), (1,)), ((), ())), preferred_element_type=F32)


def along_y(a, lane, width):
    after = jnp.where(lane < width - 1, pltpu.roll(a, width - 1, 1), 0.0)
    before = jnp.where(lane > 0, pltpu.roll(a, 1, 1), 0.0)
    return after - before


def updated_stress(sig, dz, dx, dy, elastic, cone):
    half = 0.5 * DT
    common = half * (dz[0] + dx[1] + dy[2])
    trial = [
        sig[0] + DT * dz[0] + common,
        sig[1] + DT * dx[1] + common,
        sig[2] + DT * dy[2] + common,
        sig[3] + half * (dx[0] + dz[1]),
        sig[4] + half * (dy[0] + dz[2]),
        sig[5] + half * (dy[1] + dx[2]),
    ]
    pressure = (trial[0] + trial[1] + trial[2]) * (1.0 / 3.0)
    dev = [trial[i] - pressure for i in range(3)]
    second = 0.5 * (dev[0] * dev[0] + dev[1] * dev[1] + dev[2] * dev[2]) + (
        trial[3] * trial[3] + trial[4] * trial[4] + trial[5] * trial[5]
    )
    shrink = 1.0 / (1.0 + 1.5 * jnp.sqrt(second))
    factor = jnp.where(elastic, 1.0, jnp.where(cone, shrink, 0.0))
    new = [dev[i] * factor + pressure for i in range(3)]
    return new + [trial[i] * factor for i in range(3, 6)]


def kernel(
    sizes,
    stress,
    velocity,
    density,
    flags,
    pile0,
    mass,
    jack,
    pair_elem,
    pair_cell,
    stress_out,
    velocity_out,
    pile_out,
    sig,
    vx,
    v0,
    scale,
    flg,
    sigp,
    spk,
    pbuf,
    rxp,
    cbuf,
    crx,
    pvw,
    massv,
    jackv,
    pilev,
    jackw,
    elemv,
    cellv,
    crow,
    prow,
    acol,
    arow,
    bcol,
    brow,
    thi,
    tlo,
    phi,
    plo,
    acc_s,
    acc_c,
    count_c,
    sbuf,
    sdep,
    sown,
    rx,
    nbuf,
    ndep,
    nsum,
    rxn,
    nown,
    local_sem,
    init_send,
    init_recv,
    halo_send,
    halo_recv,
    dep_send,
    dep_recv,
    part_send,
    part_recv,
    num_send,
    num_recv,
    all_send,
    all_recv,
    leg_send,
    leg_recv,
    win_send,
    win_recv,
):
    depth_count, plan_count, cz, cx, cy, tiles, pairs, chunk = sizes
    units = 3 * tiles
    slots = -(-units // plan_count)
    rows = cz * cx
    prows = brow.shape[0]
    block_rows = tiles // 2 * 8
    d = lax.axis_index("depth")
    p = lax.axis_index("plan")
    d_up = lax.rem(d + 1, depth_count)
    d_dn = lax.rem(d + depth_count - 1, depth_count)
    p_up = lax.rem(p + 1, plan_count)
    p_dn = lax.rem(p + plan_count - 1, plan_count)
    own = pl.ds(8, cx)
    y_count = plan_count // 2
    y = p // 2
    z_low = p % 2
    odd = d % 2
    d_near = d + 1 - 2 * odd
    d_far = lax.rem(d + depth_count - 1 + 2 * odd, depth_count)
    kinds = ((d_far, 2 * odd), (d_near, 2 - 2 * odd), (d, 1))

    def everyone(first, visit):
        def body(i, unused):
            step = (i + 1) // 2
            yy = lax.rem(y + y_count // 2 + step * (1 - 2 * (i % 2)) + y_count, y_count)
            for kind in range(first, 3):
                dd, block = kinds[kind]
                for z in (1 - z_low, z_low):
                    act = functools.partial(visit, kind, dd, block, yy * 2 + z)
                    if kind == 2 and z is z_low:
                        pl.when(i < y_count - 1)(act)
                    else:
                        act()
            return unused

        lax.fori_loop(0, y_count, body, 0)

    def remote(src, dst, send, recv, dd, pp):
        return pltpu.make_async_remote_copy(
            src_ref=src,
            dst_ref=dst,
            send_sem=send,
            recv_sem=recv,
            device_id={"depth": dd, "plan": pp},
            device_id_type=MESH,
        )

    local = [
        (stress, sig.at[:, pl.ds(1, cz), own, :]),
        (velocity, v0),
        (density, scale),
        (flags, flg.at[pl.ds(1, cz)]),
        (pile0, pilev),
        (mass, massv),
        (jack, jackw),
        (pair_elem, elemv),
        (pair_cell, cellv),
    ]
    local = [
        pltpu.make_async_copy(src, dst, local_sem.at[i]) for i, (src, dst) in enumerate(local)
    ]
    for copy in local:
        copy.start()

    barrier = pltpu.get_barrier_semaphore()
    corners = ((d_dn, p_dn), (d_dn, p_up), (d_up, p_dn), (d_up, p_up))

    def greet(kind, dd, block, q):
        pl.semaphore_signal(
            barrier, inc=1, device_id={"depth": dd, "plan": q}, device_id_type=MESH
        )

    everyone(2, greet)
    for dd, pp in ((d_dn, p), (d_up, p)) + corners:
        greet(0, dd, 1, pp)
    for i in (0, 3):
        local[i].wait()

    def pack_edges(z, unused):
        at = pl.ds(z, 1)
        for c in range(6):
            spk[0, c, at, :] = sig[c, z + 1, 8:9, :]
            spk[1, c, at, :] = sig[c, z + 1, cx + 7 : cx + 8, :]
        spk[0, 6, at, :] = flg[z + 1, 0:1, :].astype(F32)
        spk[1, 6, at, :] = flg[z + 1, cx - 1 : cx, :].astype(F32)
        return unused

    lax.fori_loop(0, cz, pack_edges, 0)

    local[4].wait()
    local[6].wait()

    def pile_tiles(t, unused):
        for r in range(8):
            at = pl.ds(pl.multiple_of(t * 1024 + r * 128, 128), 128)
            for source, target, first in ((pilev, pvw.at[0], units), (jackw, jackv, 0)):
                value = source[:, at]
                for c in range(3):
                    target[first + c * tiles + t, r : r + 1, :] = value[c : c + 1]
        return unused

    lax.fori_loop(0, tiles, pile_tiles, 0)
    for i in (1, 2, 5, 7, 8):
        local[i].wait()

    def tables(i, unused):
        at = pl.ds(pl.multiple_of(i * chunk, chunk), chunk)
        cell = cellv[:, at]
        elem = elemv[:, at]
        live = cell >= 0
        c_row = jnp.where(live, cell // cy, -1)
        c_col = jnp.where(live, cell % cy, -1)
        block = elem // (tiles * 1024)
        inner = elem - block * (tiles * 1024)
        half_row = inner // 128
        p_row = block * block_rows + (half_row // 16) * 8 + half_row % 8
        p_col = (half_row // 8 % 2) * 128 + inner % 128
        p_row = jnp.where(live, p_row, -1)
        crow[:, at] = c_row
        prow[:, at] = p_row
        across = lax.broadcasted_iota(jnp.int32, (cy, chunk), 0)
        acol[:, at] = (across == c_col).astype(F32).astype(BF16)
        arow[:, at] = (across[:rows] == c_row).astype(F32).astype(BF16)
        wide = lax.broadcasted_iota(jnp.int32, (256, chunk), 0)
        bcol[:, at] = (wide == p_col).astype(F32).astype(BF16)
        brow[:, at] = (wide[:prows] == p_row).astype(F32).astype(BF16)
        return unused

    lax.fori_loop(0, pairs // chunk, tables, 0)

    def split_start(z, unused):
        for c in range(3):
            high, low = split_two(v0[c, z])
            at = pl.ds(pl.multiple_of(c * rows + z * cx, 16), cx)
            thi[at, :] = high
            tlo[at, :] = low
        scale[z] = DT / scale[z]
        return unused

    lax.fori_loop(0, cz, split_start, 0)
    def pile_terms(s):
        acc_s[...] = jnp.zeros_like(acc_s)

        def body(i, unused):
            at = pl.ds(pl.multiple_of(i * chunk, chunk), chunk)
            col = acol[:, at]
            picked = dot_nn(thi[...], col) + dot_nn(tlo[...], col)
            here = lax.broadcasted_iota(jnp.int32, (rows, chunk), 0) == crow[:, at]
            row = brow[:, at]
            high, low = [], []
            for c in range(3):
                value = jnp.sum(
                    jnp.where(here, picked[c * rows : (c + 1) * rows], 0.0), axis=0, keepdims=True
                )
                first, second = split_two(value)
                high.append(row * first)
                low.append(row * second)
            wide = bcol[:, at]
            acc_s[...] += dot_nt(jnp.concatenate(high, 0), wide) + dot_nt(
                jnp.concatenate(low, 0), wide
            )
            return unused

        lax.fori_loop(0, pairs // chunk, body, 0, unroll=True)
        for b in range(3):
            for c in range(3):
                for t in range(tiles):
                    r = c * prows + b * block_rows + t // 2 * 8
                    l = t % 2 * 128
                    sbuf[s, b, c * tiles + t] = acc_s[r : r + 8, l : l + 128]

    def cell_terms(s):
        for b in range(3):
            for c in range(3):
                for a in range(tiles // 2):
                    u = b * units + c * tiles + 2 * a
                    r = c * prows + b * block_rows + a * 8
                    phi[r : r + 8, 0:128] = pvw[s, u]
                    phi[r : r + 8, 128:256] = pvw[s, u + 1]
        high, low = split_two(phi[...])
        plo[0] = high
        plo[1] = low

        picked = dot_nn(plo[0], bcol[...]) + dot_nn(plo[1], bcol[...])
        here = lax.broadcasted_iota(jnp.int32, (prows, pairs), 0) == prow[...]
        high, low = [], []
        for c in range(3):
            value = jnp.sum(
                jnp.where(here, picked[c * prows : (c + 1) * prows], 0.0), axis=0, keepdims=True
            )
            first, second = split_two(value)
            high.append(arow[...] * first)
            low.append(arow[...] * second)
        acc_c[...] = dot_nt(jnp.concatenate(high, 0), acol[...]) + dot_nt(
            jnp.concatenate(low, 0), acol[...]
        )


    count_c[...] = dot_nt(arow[...], acol[...])
    acc_s[0:prows, :] = dot_nt(brow[...], bcol[...])
    for b in range(3):
        for t in range(tiles):
            r = b * block_rows + t // 2 * 8
            l = t % 2 * 128
            nbuf[b, t] = acc_s[r : r + 8, l : l + 128]
    phi[...] = jnp.zeros_like(phi)
    pile_terms(0)
    pl.semaphore_wait(barrier, plan_count + 5)
    mine = pl.ds(units, units)
    init = [
        remote(
            nbuf.at[0], ndep.at[1], dep_send.at[0], dep_recv.at[0], d_dn, p
        ),
        remote(
            nbuf.at[2], ndep.at[0], dep_send.at[1], dep_recv.at[1], d_up, p
        ),
        remote(
            pvw.at[0, mine],
            pvw.at[0, pl.ds(0, units)],
            init_send.at[0],
            init_recv.at[0],
            d_up,
            p,
        ),
        remote(
            pvw.at[0, mine],
            pvw.at[0, pl.ds(2 * units, units)],
            init_send.at[1],
            init_recv.at[1],
            d_dn,
            p,
        ),
        remote(
            stress.at[:, cz - 1], sig.at[:, 0, own, :], init_send.at[2], init_recv.at[2], d_up, p
        ),
        remote(
            stress.at[:, 0], sig.at[:, cz + 1, own, :], init_send.at[3], init_recv.at[3], d_dn, p
        ),
        remote(spk.at[0], sigp.at[1], init_send.at[4], init_recv.at[4], d, p_dn),
        remote(spk.at[1], sigp.at[0], init_send.at[5], init_recv.at[5], d, p_up),
        remote(flags.at[cz - 1], flg.at[0], init_send.at[6], init_recv.at[6], d_up, p),
        remote(flags.at[0], flg.at[cz + 1], init_send.at[7], init_recv.at[7], d_dn, p),
    ]

    def depth_leg(s):
        return [
            remote(sbuf.at[s, 0], sdep.at[s, 1], leg_send.at[s, 0], leg_recv.at[s, 0], d_dn, p),
            remote(sbuf.at[s, 2], sdep.at[s, 0], leg_send.at[s, 1], leg_recv.at[s, 1], d_up, p),
        ]

    def window_leg(s):
        block = lambda b: pvw.at[s + 1, pl.ds(b * units, units)]
        return [
            remote(block(1), block(0), win_send.at[s, 0], win_recv.at[s, 0], d_up, p),
            remote(block(1), block(2), win_send.at[s, 1], win_recv.at[s, 1], d_dn, p),
        ]

    def owned(j, q, work):
        if plan_count * (j + 1) <= units:
            work()
        else:
            pl.when(q + plan_count * j < units)(work)

    def send_parts(s):
        def visit(kind, dd, block, q):
            for j in range(slots):
                u = q + plan_count * j
                source = sown.at[s, u] if s in SUMS_IN_TWO else sbuf.at[s, block, u]
                owned(
                    j,
                    q,
                    lambda: remote(
                        source,
                        rx.at[s, j, kind * plan_count + p],
                        part_send.at[s, j],
                        part_recv.at[s, j],
                        dd,
                        q,
                    ).start(),
                )

        everyone(2 if s in SUMS_IN_TWO else 0, visit)

    def start_parts(s):
        if s in SUMS_IN_TWO:
            for copy in depth_leg(s):
                copy.start()
        else:
            send_parts(s)

    def middle_parts(s):
        if s in SUMS_IN_TWO:
            for copy in depth_leg(s):
                copy.wait_recv()
            for u in range(units):
                sown[s, u] = sbuf[s, 1, u] + sdep[s, 0, u] + sdep[s, 1, u]
            send_parts(s)

    def start_numbers():
        for t in range(tiles):
            nsum[t] = nbuf[1, t] + ndep[0, t] + ndep[1, t]

        def visit(kind, dd, block, q):
            for j in range(slots):
                owned(
                    j,
                    q,
                    lambda: remote(
                        nsum.at[lax.rem(q + plan_count * j, tiles)],
                        rxn.at[j, p],
                        num_send.at[j],
                        num_recv.at[j],
                        d,
                        q,
                    ).start(),
                )

        everyone(2, visit)

    def some_of(ref, number, send, recv):
        some = ref.at[pl.ds(0, number)]
        return remote(some, some, send, recv, d, p_up)

    def parts_wait(s, j, number):
        return some_of(rx.at[s, j], number, part_send.at[s, j], part_recv.at[s, j])

    def numbers_wait(j, number):
        return some_of(rxn.at[j], number, num_send.at[j], num_recv.at[j])

    def all_wait(s, j, number):
        return some_of(pvw.at[s + 1], number, all_send.at[s, j], all_recv.at[s, j])

    def not_mine(j, many, act):
        here = min(plan_count, units - plan_count * j)
        if here == plan_count:
            act(here * many - 1)
        else:
            if here * many > 1:
                pl.when(p < here)(lambda: act(here * many - 1))
            pl.when(p >= here)(lambda: act(here * many))

    def update_pile(s):
        first = 2 if s in TILES_IN_TWO or s == STEPS - 1 else 0
        two = s in SUMS_IN_TWO
        for j in range(slots):
            u = p + plan_count * j

            def work():
                t = lax.rem(u, tiles)
                parts_wait(s, j, (1 if two else 3) * plan_count - 1).wait_recv()
                rx[s, j, 2 * plan_count + p] = sown[s, u] if two else sbuf[s, 1, u]
                if s == 0:
                    numbers_wait(j, plan_count - 1).wait_recv()
                    rxn[j, p] = nsum[t]
                    nown[j] = jnp.sum(rxn[j], axis=0)
                before = pvw[s, units + u]
                force = jackv[u] + jnp.sum(rx[s, j, (2 * plan_count if two else 0) :], axis=0) - nown[j] * before
                pvw[s + 1, units + u] = before + DT * force / massv[t]

                def visit(kind, dd, block, q):
                    remote(
                        pvw.at[s + 1, units + u],
                        pvw.at[s + 1, (2 - block) * units + u],
                        all_send.at[s, j],
                        all_recv.at[s, j],
                        dd,
                        q,
                    ).start()

                everyone(first, visit)

            owned(j, p, work)

    def own_pile(s):
        if s in TILES_IN_TWO:
            for j in range(slots):
                not_mine(j, 1, lambda number: all_wait(s, j, number).wait_recv())
            for copy in window_leg(s):
                copy.start()

    def wait_pile(s):
        if s in TILES_IN_TWO:
            for copy in window_leg(s):
                copy.wait_recv()
            return
        many = 3 if s < STEPS - 1 else 1
        for j in range(slots):
            not_mine(j, many, lambda number: all_wait(s, j, number).wait_recv())

    def drain_pile(s):
        many = 1 if s in TILES_IN_TWO or s == STEPS - 1 else 3
        sums = 1 if s in SUMS_IN_TWO else 3
        if s in SUMS_IN_TWO:
            for copy in depth_leg(s):
                copy.wait_send()
        if s in TILES_IN_TWO:
            for copy in window_leg(s):
                copy.wait_send()
        for j in range(slots):
            not_mine(j, sums, lambda number: parts_wait(s, j, number).wait_send())
            if s == 0:
                not_mine(j, 1, lambda number: numbers_wait(j, number).wait_send())
            owned(j, p, lambda: all_wait(s, j, many * plan_count - 1).wait_send())

    lane = lax.broadcasted_iota(jnp.int32, (cx, cy), 1)
    lane_p = lax.broadcasted_iota(jnp.int32, (cz, cy), 1)

    def new_velocity(s):
        def body(z, unused):
            for c in (1, 3, 5):
                sig[c, z + 1, 7:8, :] = sigp[0, c, pl.ds(z, 1), :]
                sig[c, z + 1, cx + 8 : cx + 9, :] = sigp[1, c, pl.ds(z, 1), :]
            for c in range(3):
                i, j, k = SYM[c]
                force = sig[i, z + 2, own, :] - sig[i, z, own, :]
                force += sig[j, z + 1, pl.ds(9, cx), :] - sig[j, z + 1, pl.ds(7, cx), :]
                force += along_y(sig[k, z + 1, own, :], lane, cy)
                old = v0[c, z] if s == 0 else vx[s - 1, c, z + 2, own, :]
                at = pl.ds(pl.multiple_of(z * cx, 16), cx)
                spot = pl.ds(pl.multiple_of(c * rows + z * cx, 16), cx)
                push = acc_c[spot, :] - count_c[at, :] * old
                new = old + scale[z] * (0.5 * force + push)
                vx[s, c, z + 2, own, :] = new
                if s < STEPS - 1:
                    high, low = split_two(new)
                    thi[spot, :] = high
                    tlo[spot, :] = low
                row = pl.ds(z, 1)
                pbuf[s, 0, c, 0, row, :] = new[0:1]
                pbuf[s, 1, c, 1, row, :] = new[cx - 1 : cx]
                if s < STEPS - 1:
                    pbuf[s, 0, c, 1, row, :] = new[1:2]
                    pbuf[s, 1, c, 0, row, :] = new[cx - 2 : cx - 1]
            return unused

        lax.fori_loop(0, cz, body, 0)
        if s < STEPS - 1:
            for i in range(4):
                z = cz - 1 if i // 2 else 0
                x = cx - 1 if i % 2 else 0
                for c in range(3):
                    cbuf[s, i, c : c + 1, :] = vx[s, c, z + 2, 8 + x : 9 + x, :]

    def halo_leg(s):
        w = 2 if s < STEPS - 1 else 1
        xs0 = pl.ds(0, w)
        xs1 = pl.ds(2 - w, w)
        mid = pl.ds(8, cz)
        send = lambda i: (halo_send.at[s, i], halo_recv.at[s, i])
        copies = []
        if s < STEPS - 1:
            for i in range(4):
                copies.append(remote(cbuf.at[s, i], crx.at[s, i], *send(4 + i), *corners[i]))
        copies += [
            remote(
                vx.at[s, :, pl.ds(cz + 2 - w, w), own, :],
                vx.at[s, :, pl.ds(2 - w, w), own, :],
                *send(0),
                d_up,
                p,
            ),
            remote(
                vx.at[s, :, pl.ds(2, w), own, :],
                vx.at[s, :, pl.ds(cz + 2, w), own, :],
                *send(1),
                d_dn,
                p,
            ),
            remote(pbuf.at[s, 0, :, xs0], rxp.at[s, 1, :, xs0, mid, :], *send(2), d, p_dn),
            remote(pbuf.at[s, 1, :, xs1], rxp.at[s, 0, :, xs1, mid, :], *send(3), d, p_up),
        ]
        return copies

    def new_stress(s):
        last = s == STEPS - 1

        @pl.when(d == 0)
        def _():
            vx[s, :, 0:2, own, :] = jnp.zeros((3, 2, cx, cy), F32)
            if not last:
                crx[s, 2:4] = jnp.zeros((2, 3, cy), F32)

        @pl.when(d == depth_count - 1)
        def _():
            vx[s, :, cz + 2 : cz + 4, own, :] = jnp.zeros((3, 2, cx, cy), F32)
            if not last:
                crx[s, 0:2] = jnp.zeros((2, 3, cy), F32)

        @pl.when(p == 0)
        def _():
            rxp[s, 0, :, :, 8 : 8 + cz, :] = jnp.zeros((3, 2, cz, cy), F32)
            if not last:
                for i in (1, 3):
                    crx[s, i] = jnp.zeros((3, cy), F32)

        @pl.when(p == plan_count - 1)
        def _():
            rxp[s, 1, :, :, 8 : 8 + cz, :] = jnp.zeros((3, 2, cz, cy), F32)
            if not last:
                for i in (0, 2):
                    crx[s, i] = jnp.zeros((3, cy), F32)

        if not last:
            for c in range(3):
                for side in range(2):
                    x = 7 if side == 0 else cx + 8
                    below = crx[s, 3 - side, c : c + 1, :]
                    above = crx[s, 1 - side, c : c + 1, :]
                    vx[s, c, 1, x : x + 1, :] = below
                    vx[s, c, cz + 2, x : x + 1, :] = above
                    rxp[s, side, c, 1 - side, 7:8, :] = below
                    rxp[s, side, c, 1 - side, cz + 8 : cz + 9, :] = above

        def rows_in(z, unused):
            for c in range(3):
                vx[s, c, z + 2, 7:8, :] = rxp[s, 0, c, 1, pl.ds(z + 8, 1), :]
                vx[s, c, z + 2, cx + 8 : cx + 9, :] = rxp[s, 1, c, 0, pl.ds(z + 8, 1), :]
            return unused

        lax.fori_loop(0, cz, rows_in, 0)

        def body(layer, unused):
            dz = [
                vx[s, c, layer + 2, own, :] - vx[s, c, layer, own, :] for c in range(3)
            ]
            dx = [
                vx[s, c, layer + 1, pl.ds(9, cx), :] - vx[s, c, layer + 1, pl.ds(7, cx), :]
                for c in range(3)
            ]
            dy = [along_y(vx[s, c, layer + 1, own, :], lane, cy) for c in range(3)]
            flag = flg[layer]
            new = updated_stress(
                [sig[c, layer, own, :] for c in range(6)], dz, dx, dy, flag == 0, flag == 1
            )
            for c in range(6):
                sig[c, layer, own, :] = new[c]
            return unused

        if last:
            lax.fori_loop(1, cz + 1, body, 0)
            return
        lax.fori_loop(0, cz + 2, body, 0)
        for side in range(2):
            inner = [pbuf[s, side, c, side] for c in range(3)]
            outer = [rxp[s, side, c, side, 8 : 8 + cz, :] for c in range(3)]
            sign = 1.0 if side == 0 else -1.0
            ring = 1 - side
            dz = [
                rxp[s, side, c, ring, 9 : 9 + cz, :] - rxp[s, side, c, ring, 7 : 7 + cz, :]
                for c in range(3)
            ]
            dx = [sign * (inner[c] - outer[c]) for c in range(3)]
            dy = [along_y(rxp[s, side, c, ring, 8 : 8 + cz, :], lane_p, cy) for c in range(3)]
            flag = sigp[side, 6]
            new = updated_stress(
                [sigp[side, c] for c in range(6)], dz, dx, dy, flag == 0.0, flag == 1.0
            )
            for c in range(6):
                sigp[side, c] = new[c]
        clear_outside()

    def clear_outside():
        @pl.when(d == 0)
        def _():
            sig[:, 0, own, :] = jnp.zeros((6, cx, cy), F32)

        @pl.when(d == depth_count - 1)
        def _():
            sig[:, cz + 1, own, :] = jnp.zeros((6, cx, cy), F32)

        @pl.when(p == 0)
        def _():
            sigp[0, 0:6] = jnp.zeros((6, cz, cy), F32)

        @pl.when(p == plan_count - 1)
        def _():
            sigp[1, 0:6] = jnp.zeros((6, cz, cy), F32)

    def start(copies):
        for copy in copies:
            copy.start()
        return copies

    def arrive(copies):
        for copy in copies:
            copy.wait_recv()

    start(init[0:2])
    start_parts(0)
    start(init[2:])
    arrive(init[0:2])
    start_numbers()
    middle_parts(0)
    arrive(init[2:4])
    cell_terms(0)
    arrive(init[4:])
    clear_outside()
    new_velocity(0)
    halos = [start(halo_leg(0))]
    pile_terms(1)
    start_parts(1)
    update_pile(0)
    middle_parts(1)
    own_pile(0)
    arrive(halos[0])
    new_stress(0)
    update_pile(1)
    wait_pile(0)
    cell_terms(1)
    new_velocity(1)
    halos.append(start(halo_leg(1)))
    pile_terms(2)
    start_parts(2)
    own_pile(1)
    middle_parts(2)
    arrive(halos[1])
    new_stress(1)
    wait_pile(1)
    cell_terms(2)
    new_velocity(2)
    halos.append(start(halo_leg(2)))
    velocity_back = pltpu.make_async_copy(
        vx.at[2, :, pl.ds(2, cz), own, :], velocity_out, local_sem.at[0]
    )
    velocity_back.start()
    update_pile(2)
    arrive(halos[2])
    new_stress(2)
    stress_back = pltpu.make_async_copy(
        sig.at[:, pl.ds(1, cz), own, :], stress_out, local_sem.at[1]
    )
    stress_back.start()
    wait_pile(2)

    def pile_lines(t, unused):
        for r in range(8):
            at = pl.ds(pl.multiple_of(t * 1024 + r * 128, 128), 128)
            for c in range(3):
                pilev[c : c + 1, at] = pvw[STEPS, units + c * tiles + t, r : r + 1, :]
        return unused

    lax.fori_loop(0, tiles, pile_lines, 0)
    pile_back = pltpu.make_async_copy(pilev, pile_out, local_sem.at[2])
    pile_back.start()

    for copies in [init] + halos:
        for copy in copies:
            copy.wait_send()
    for s in range(STEPS):
        drain_pile(s)
    velocity_back.wait()
    stress_back.wait()
    pile_back.wait()


def shards(
    depth_count,
    plan_count,
    stress,
    velocity,
    density,
    flags,
    pile_velocity,
    pile_mass,
    jack_force,
    pair_elem,
    pair_cell,
):
    cz, cx, cy = density.shape
    width = pile_mass.shape[0]
    tiles = width // 1024
    pairs = pair_elem.shape[1]
    chunk = min(1024, pairs)
    units = 3 * tiles
    slots = -(-units // plan_count)
    rows = cz * cx
    prows = -(-(3 * width // 256) // 16) * 16
    sizes = (depth_count, plan_count, cz, cx, cy, tiles, pairs, chunk)
    vm = lambda *shape: pltpu.VMEM(shape, F32)
    half = lambda *shape: pltpu.VMEM(shape, BF16)
    whole = lambda *shape: pltpu.VMEM(shape, jnp.int32)
    dma = lambda *shape: pltpu.SemaphoreType.DMA(shape)
    scratch = [
        vm(6, cz + 2, cx + 16, cy),
        vm(STEPS, 3, cz + 4, cx + 16, cy),
        vm(3, cz, cx, cy),
        vm(cz, cx, cy),
        whole(cz + 2, cx, cy),
        vm(2, 7, cz, cy),
        vm(2, 7, cz, cy),
        vm(STEPS, 2, 3, 2, cz, cy),
        vm(STEPS, 2, 3, 2, cz + 16, cy),
        vm(STEPS, 4, 3, cy),
        vm(STEPS, 4, 3, cy),
        vm(STEPS + 1, 3 * units, 8, 128),
        vm(tiles, 8, 128),
        vm(units, 8, 128),
        vm(3, width),
        vm(3, width),
        whole(1, pairs),
        whole(1, pairs),
        whole(1, pairs),
        whole(1, pairs),
        half(cy, pairs),
        half(rows, pairs),
        half(256, pairs),
        half(prows, pairs),
        half(3 * rows, cy),
        half(3 * rows, cy),
        vm(3 * prows, 256),
        half(2, 3 * prows, 256),
        vm(3 * prows, 256),
        vm(3 * rows, cy),
        vm(rows, cy),
        vm(STEPS, 3, units, 8, 128),
        vm(STEPS, 2, units, 8, 128),
        vm(STEPS, units, 8, 128),
        vm(STEPS, slots, 3 * plan_count, 8, 128),
        vm(3, tiles, 8, 128),
        vm(2, tiles, 8, 128),
        vm(tiles, 8, 128),
        vm(slots, plan_count, 8, 128),
        vm(slots, 8, 128),
        dma(9),
        dma(8),
        dma(8),
        dma(STEPS, 8),
        dma(STEPS, 8),
        dma(2),
        dma(2),
        dma(STEPS, slots),
        dma(STEPS, slots),
        dma(slots),
        dma(slots),
        dma(STEPS, slots),
        dma(STEPS, slots),
        dma(STEPS, 2),
        dma(STEPS, 2),
        dma(STEPS, 2),
        dma(STEPS, 2),
    ]
    anywhere = pl.BlockSpec(memory_space=pl.ANY)
    stress, velocity, pile = pl.pallas_call(
        functools.partial(kernel, sizes),
        out_shape=(
            jax.ShapeDtypeStruct(stress.shape, F32),
            jax.ShapeDtypeStruct(velocity.shape, F32),
            jax.ShapeDtypeStruct((3, width), F32),
        ),
        in_specs=[anywhere] * 9,
        out_specs=(anywhere,) * 3,
        scratch_shapes=scratch,
        compiler_params=pltpu.CompilerParams(
            collective_id=0, has_side_effects=True, vmem_limit_bytes=60 * 1024 * 1024
        ),
    )(
        stress,
        velocity,
        density,
        flags,
        pile_velocity,
        pile_mass.reshape(tiles, 8, 128),
        jack_force,
        pair_elem,
        pair_cell,
    )
    return stress, velocity, pile


def solution(mesh):
    field = P(None, "depth", "plan", None)
    cells = P("depth", "plan", None)
    placed = (
        field,
        field,
        cells,
        cells,
        P(None, "depth"),
        P("depth"),
        P(None, "depth"),
        P("depth", "plan"),
        P("depth", "plan"),
    )
    return jax.shard_map(
        functools.partial(shards, mesh.shape["depth"], mesh.shape["plan"]),
        mesh=mesh,
        in_specs=placed,
        out_specs=(field, field, P(None, "depth")),
        check_vma=False,
    )
```

```python
import functools

import jax
import jax.numpy as jnp
from jax import lax
from jax.experimental import pallas as pl
from jax.experimental.pallas import tpu as pltpu
from jax.sharding import PartitionSpec as P

STEPS = 3
DT = 0.2
MESH = pl.DeviceIdType.MESH
F32 = jnp.float32
BF16 = jnp.bfloat16
SYM = ((0, 3, 4), (3, 1, 5), (4, 5, 2))
SUMS_IN_TWO = (0, 1, 2)
TILES_IN_TWO = (0, 1)


def split_two(x):
    high = x.astype(BF16)
    return high, (x - high.astype(F32)).astype(BF16)


def dot_nn(a, b):
    return jnp.dot(a, b, preferred_element_type=F32)


def dot_nt(a, b):
    return lax.dot_general(a, b, (((1,), (1,)), ((), ())), preferred_element_type=F32)


def along_y(a, lane, width):
    after = jnp.where(lane < width - 1, pltpu.roll(a, width - 1, 1), 0.0)
    before = jnp.where(lane > 0, pltpu.roll(a, 1, 1), 0.0)
    return after - before


def updated_stress(sig, dz, dx, dy, elastic, cone):
    half = 0.5 * DT
    common = half * (dz[0] + dx[1] + dy[2])
    trial = [
        sig[0] + DT * dz[0] + common,
        sig[1] + DT * dx[1] + common,
        sig[2] + DT * dy[2] + common,
        sig[3] + half * (dx[0] + dz[1]),
        sig[4] + half * (dy[0] + dz[2]),
        sig[5] + half * (dy[1] + dx[2]),
    ]
    pressure = (trial[0] + trial[1] + trial[2]) * (1.0 / 3.0)
    dev = [trial[i] - pressure for i in range(3)]
    second = 0.5 * (dev[0] * dev[0] + dev[1] * dev[1] + dev[2] * dev[2]) + (
        trial[3] * trial[3] + trial[4] * trial[4] + trial[5] * trial[5]
    )
    shrink = 1.0 / (1.0 + 1.5 * jnp.sqrt(second))
    factor = jnp.where(elastic, 1.0, jnp.where(cone, shrink, 0.0))
    new = [dev[i] * factor + pressure for i in range(3)]
    return new + [trial[i] * factor for i in range(3, 6)]


def kernel(
    sizes,
    stress,
    velocity,
    density,
    flags,
    pile0,
    mass,
    jack,
    pair_elem,
    pair_cell,
    stress_out,
    velocity_out,
    pile_out,
    sig,
    vx,
    v0,
    scale,
    flg,
    sigp,
    spk,
    pbuf,
    rxp,
    cbuf,
    crx,
    pvw,
    massv,
    jackv,
    pilev,
    jackw,
    elemv,
    cellv,
    crow,
    prow,
    acol,
    arow,
    bcol,
    brow,
    thi,
    tlo,
    phi,
    plo,
    acc_s,
    acc_c,
    count_c,
    sbuf,
    sdep,
    sown,
    rx,
    nbuf,
    ndep,
    nsum,
    rxn,
    nown,
    local_sem,
    init_send,
    init_recv,
    halo_send,
    halo_recv,
    dep_send,
    dep_recv,
    part_send,
    part_recv,
    num_send,
    num_recv,
    all_send,
    all_recv,
    leg_send,
    leg_recv,
    win_send,
    win_recv,
):
    depth_count, plan_count, cz, cx, cy, tiles, pairs, chunk = sizes
    units = 3 * tiles
    slots = -(-units // plan_count)
    rows = cz * cx
    prows = brow.shape[0]
    block_rows = tiles // 2 * 8
    d = lax.axis_index("depth")
    p = lax.axis_index("plan")
    d_up = lax.rem(d + 1, depth_count)
    d_dn = lax.rem(d + depth_count - 1, depth_count)
    p_up = lax.rem(p + 1, plan_count)
    p_dn = lax.rem(p + plan_count - 1, plan_count)
    own = pl.ds(8, cx)
    y_count = plan_count // 2
    y = p // 2
    z_low = p % 2
    odd = d % 2
    d_near = d + 1 - 2 * odd
    d_far = lax.rem(d + depth_count - 1 + 2 * odd, depth_count)
    kinds = ((d_far, 2 * odd), (d_near, 2 - 2 * odd), (d, 1))

    def everyone(first, visit):
        def body(i, unused):
            step = (i + 1) // 2
            yy = lax.rem(y + y_count // 2 + step * (1 - 2 * (i % 2)) + y_count, y_count)
            for kind in range(first, 3):
                dd, block = kinds[kind]
                for z in (1 - z_low, z_low):
                    act = functools.partial(visit, kind, dd, block, yy * 2 + z)
                    if kind == 2 and z is z_low:
                        pl.when(i < y_count - 1)(act)
                    else:
                        act()
            return unused

        lax.fori_loop(0, y_count, body, 0)

    def remote(src, dst, send, recv, dd, pp):
        return pltpu.make_async_remote_copy(
            src_ref=src,
            dst_ref=dst,
            send_sem=send,
            recv_sem=recv,
            device_id={"depth": dd, "plan": pp},
            device_id_type=MESH,
        )

    local = [
        (stress, sig.at[:, pl.ds(1, cz), own, :]),
        (velocity, v0),
        (density, scale),
        (flags, flg.at[pl.ds(1, cz)]),
        (pile0, pilev),
        (mass, massv),
        (jack, jackw),
        (pair_elem, elemv),
        (pair_cell, cellv),
    ]
    local = [
        pltpu.make_async_copy(src, dst, local_sem.at[i]) for i, (src, dst) in enumerate(local)
    ]
    for copy in local:
        copy.start()

    barrier = pltpu.get_barrier_semaphore()
    corners = ((d_dn, p_dn), (d_dn, p_up), (d_up, p_dn), (d_up, p_up))

    def greet(kind, dd, block, q):
        pl.semaphore_signal(
            barrier, inc=1, device_id={"depth": dd, "plan": q}, device_id_type=MESH
        )

    everyone(2, greet)
    for dd, pp in ((d_dn, p), (d_up, p)) + corners:
        greet(0, dd, 1, pp)
    for i in (0, 3):
        local[i].wait()

    def pack_edges(z, unused):
        at = pl.ds(z, 1)
        for c in range(6):
            spk[0, c, at, :] = sig[c, z + 1, 8:9, :]
            spk[1, c, at, :] = sig[c, z + 1, cx + 7 : cx + 8, :]
        spk[0, 6, at, :] = flg[z + 1, 0:1, :].astype(F32)
        spk[1, 6, at, :] = flg[z + 1, cx - 1 : cx, :].astype(F32)
        return unused

    lax.fori_loop(0, cz, pack_edges, 0)

    local[4].wait()
    local[6].wait()

    def pile_tiles(t, unused):
        for r in range(8):
            at = pl.ds(pl.multiple_of(t * 1024 + r * 128, 128), 128)
            for source, target, first in ((pilev, pvw.at[0], units), (jackw, jackv, 0)):
                value = source[:, at]
                for c in range(3):
                    target[first + c * tiles + t, r : r + 1, :] = value[c : c + 1]
        return unused

    lax.fori_loop(0, tiles, pile_tiles, 0)
    for i in (1, 2, 5, 7, 8):
        local[i].wait()

    def tables(i, unused):
        at = pl.ds(pl.multiple_of(i * chunk, chunk), chunk)
        cell = cellv[:, at]
        elem = elemv[:, at]
        live = cell >= 0
        c_row = jnp.where(live, cell // cy, -1)
        c_col = jnp.where(live, cell % cy, -1)
        block = elem // (tiles * 1024)
        inner = elem - block * (tiles * 1024)
        half_row = inner // 128
        p_row = block * block_rows + (half_row // 16) * 8 + half_row % 8
        p_col = (half_row // 8 % 2) * 128 + inner % 128
        p_row = jnp.where(live, p_row, -1)
        crow[:, at] = c_row
        prow[:, at] = p_row
        across = lax.broadcasted_iota(jnp.int32, (cy, chunk), 0)
        acol[:, at] = (across == c_col).astype(F32).astype(BF16)
        arow[:, at] = (across[:rows] == c_row).astype(F32).astype(BF16)
        wide = lax.broadcasted_iota(jnp.int32, (256, chunk), 0)
        bcol[:, at] = (wide == p_col).astype(F32).astype(BF16)
        brow[:, at] = (wide[:prows] == p_row).astype(F32).astype(BF16)
        return unused

    lax.fori_loop(0, pairs // chunk, tables, 0)

    def split_start(z, unused):
        for c in range(3):
            high, low = split_two(v0[c, z])
            at = pl.ds(pl.multiple_of(c * rows + z * cx, 16), cx)
            thi[at, :] = high
            tlo[at, :] = low
        scale[z] = DT / scale[z]
        return unused

    lax.fori_loop(0, cz, split_start, 0)
    def pile_terms(s):
        acc_s[...] = jnp.zeros_like(acc_s)

        def body(i, unused):
            at = pl.ds(pl.multiple_of(i * chunk, chunk), chunk)
            col = acol[:, at]
            picked = dot_nn(thi[...], col) + dot_nn(tlo[...], col)
            here = lax.broadcasted_iota(jnp.int32, (rows, chunk), 0) == crow[:, at]
            row = brow[:, at]
            high, low = [], []
            for c in range(3):
                value = jnp.sum(
                    jnp.where(here, picked[c * rows : (c + 1) * rows], 0.0), axis=0, keepdims=True
                )
                first, second = split_two(value)
                high.append(row * first)
                low.append(row * second)
            wide = bcol[:, at]
            acc_s[...] += dot_nt(jnp.concatenate(high, 0), wide) + dot_nt(
                jnp.concatenate(low, 0), wide
            )
            return unused

        lax.fori_loop(0, pairs // chunk, body, 0, unroll=True)
        for b in range(3):
            for c in range(3):
                for t in range(tiles):
                    r = c * prows + b * block_rows + t // 2 * 8
                    l = t % 2 * 128
                    sbuf[s, b, c * tiles + t] = acc_s[r : r + 8, l : l + 128]

    def cell_terms(s):
        for b in range(3):
            for c in range(3):
                for a in range(tiles // 2):
                    u = b * units + c * tiles + 2 * a
                    r = c * prows + b * block_rows + a * 8
                    phi[r : r + 8, 0:128] = pvw[s, u]
                    phi[r : r + 8, 128:256] = pvw[s, u + 1]
        high, low = split_two(phi[...])
        plo[0] = high
        plo[1] = low

        picked = dot_nn(plo[0], bcol[...]) + dot_nn(plo[1], bcol[...])
        here = lax.broadcasted_iota(jnp.int32, (prows, pairs), 0) == prow[...]
        high, low = [], []
        for c in range(3):
            value = jnp.sum(
                jnp.where(here, picked[c * prows : (c + 1) * prows], 0.0), axis=0, keepdims=True
            )
            first, second = split_two(value)
            high.append(arow[...] * first)
            low.append(arow[...] * second)
        acc_c[...] = dot_nt(jnp.concatenate(high, 0), acol[...]) + dot_nt(
            jnp.concatenate(low, 0), acol[...]
        )


    count_c[...] = dot_nt(arow[...], acol[...])
    acc_s[0:prows, :] = dot_nt(brow[...], bcol[...])
    for b in range(3):
        for t in range(tiles):
            r = b * block_rows + t // 2 * 8
            l = t % 2 * 128
            nbuf[b, t] = acc_s[r : r + 8, l : l + 128]
    phi[...] = jnp.zeros_like(phi)
    pile_terms(0)
    pl.semaphore_wait(barrier, plan_count + 5)
    mine = pl.ds(units, units)
    init = [
        remote(
            nbuf.at[0], ndep.at[1], dep_send.at[0], dep_recv.at[0], d_dn, p
        ),
        remote(
            nbuf.at[2], ndep.at[0], dep_send.at[1], dep_recv.at[1], d_up, p
        ),
        remote(
            pvw.at[0, mine],
            pvw.at[0, pl.ds(0, units)],
            init_send.at[0],
            init_recv.at[0],
            d_up,
            p,
        ),
        remote(
            pvw.at[0, mine],
            pvw.at[0, pl.ds(2 * units, units)],
            init_send.at[1],
            init_recv.at[1],
            d_dn,
            p,
        ),
        remote(
            stress.at[:, cz - 1], sig.at[:, 0, own, :], init_send.at[2], init_recv.at[2], d_up, p
        ),
        remote(
            stress.at[:, 0], sig.at[:, cz + 1, own, :], init_send.at[3], init_recv.at[3], d_dn, p
        ),
        remote(spk.at[0], sigp.at[1], init_send.at[4], init_recv.at[4], d, p_dn),
        remote(spk.at[1], sigp.at[0], init_send.at[5], init_recv.at[5], d, p_up),
        remote(flags.at[cz - 1], flg.at[0], init_send.at[6], init_recv.at[6], d_up, p),
        remote(flags.at[0], flg.at[cz + 1], init_send.at[7], init_recv.at[7], d_dn, p),
    ]

    def depth_leg(s):
        return [
            remote(sbuf.at[s, 0], sdep.at[s, 1], leg_send.at[s, 0], leg_recv.at[s, 0], d_dn, p),
            remote(sbuf.at[s, 2], sdep.at[s, 0], leg_send.at[s, 1], leg_recv.at[s, 1], d_up, p),
        ]

    def window_leg(s):
        block = lambda b: pvw.at[s + 1, pl.ds(b * units, units)]
        return [
            remote(block(1), block(0), win_send.at[s, 0], win_recv.at[s, 0], d_up, p),
            remote(block(1), block(2), win_send.at[s, 1], win_recv.at[s, 1], d_dn, p),
        ]

    def owned(j, q, work):
        if plan_count * (j + 1) <= units:
            work()
        else:
            pl.when(q + plan_count * j < units)(work)

    def send_parts(s):
        def visit(kind, dd, block, q):
            for j in range(slots):
                u = q + plan_count * j
                source = sown.at[s, u] if s in SUMS_IN_TWO else sbuf.at[s, block, u]
                owned(
                    j,
                    q,
                    lambda: remote(
                        source,
                        rx.at[s, j, kind * plan_count + p],
                        part_send.at[s, j],
                        part_recv.at[s, j],
                        dd,
                        q,
                    ).start(),
                )

        everyone(2 if s in SUMS_IN_TWO else 0, visit)

    def start_parts(s):
        if s in SUMS_IN_TWO:
            for copy in depth_leg(s):
                copy.start()
        else:
            send_parts(s)

    def middle_parts(s):
        if s in SUMS_IN_TWO:
            for copy in depth_leg(s):
                copy.wait_recv()
            for u in range(units):
                sown[s, u] = sbuf[s, 1, u] + sdep[s, 0, u] + sdep[s, 1, u]
            send_parts(s)

    def start_numbers():
        for t in range(tiles):
            nsum[t] = nbuf[1, t] + ndep[0, t] + ndep[1, t]

        def visit(kind, dd, block, q):
            for j in range(slots):
                owned(
                    j,
                    q,
                    lambda: remote(
                        nsum.at[lax.rem(q + plan_count * j, tiles)],
                        rxn.at[j, p],
                        num_send.at[j],
                        num_recv.at[j],
                        d,
                        q,
                    ).start(),
                )

        everyone(2, visit)

    def some_of(ref, number, send, recv):
        some = ref.at[pl.ds(0, number)]
        return remote(some, some, send, recv, d, p_up)

    def parts_wait(s, j, number):
        return some_of(rx.at[s, j], number, part_send.at[s, j], part_recv.at[s, j])

    def numbers_wait(j, number):
        return some_of(rxn.at[j], number, num_send.at[j], num_recv.at[j])

    def all_wait(s, j, number):
        return some_of(pvw.at[s + 1], number, all_send.at[s, j], all_recv.at[s, j])

    def not_mine(j, many, act):
        here = min(plan_count, units - plan_count * j)
        if here == plan_count:
            act(here * many - 1)
        else:
            if here * many > 1:
                pl.when(p < here)(lambda: act(here * many - 1))
            pl.when(p >= here)(lambda: act(here * many))

    def update_pile(s):
        first = 2 if s in TILES_IN_TWO or s == STEPS - 1 else 0
        two = s in SUMS_IN_TWO
        for j in range(slots):
            u = p + plan_count * j

            def work():
                t = lax.rem(u, tiles)
                parts_wait(s, j, (1 if two else 3) * plan_count - 1).wait_recv()
                rx[s, j, 2 * plan_count + p] = sown[s, u] if two else sbuf[s, 1, u]
                if s == 0:
                    numbers_wait(j, plan_count - 1).wait_recv()
                    rxn[j, p] = nsum[t]
                    nown[j] = jnp.sum(rxn[j], axis=0)
                before = pvw[s, units + u]
                force = jackv[u] + jnp.sum(rx[s, j, (2 * plan_count if two else 0) :], axis=0) - nown[j] * before
                pvw[s + 1, units + u] = before + DT * force / massv[t]

                def visit(kind, dd, block, q):
                    remote(
                        pvw.at[s + 1, units + u],
                        pvw.at[s + 1, (2 - block) * units + u],
                        all_send.at[s, j],
                        all_recv.at[s, j],
                        dd,
                        q,
                    ).start()

                everyone(first, visit)

            owned(j, p, work)

    def own_pile(s):
        if s in TILES_IN_TWO:
            for j in range(slots):
                not_mine(j, 1, lambda number: all_wait(s, j, number).wait_recv())
            for copy in window_leg(s):
                copy.start()

    def wait_pile(s):
        if s in TILES_IN_TWO:
            for copy in window_leg(s):
                copy.wait_recv()
            return
        many = 3 if s < STEPS - 1 else 1
        for j in range(slots):
            not_mine(j, many, lambda number: all_wait(s, j, number).wait_recv())

    def drain_pile(s):
        many = 1 if s in TILES_IN_TWO or s == STEPS - 1 else 3
        sums = 1 if s in SUMS_IN_TWO else 3
        if s in SUMS_IN_TWO:
            for copy in depth_leg(s):
                copy.wait_send()
        if s in TILES_IN_TWO:
            for copy in window_leg(s):
                copy.wait_send()
        for j in range(slots):
            not_mine(j, sums, lambda number: parts_wait(s, j, number).wait_send())
            if s == 0:
                not_mine(j, 1, lambda number: numbers_wait(j, number).wait_send())
            owned(j, p, lambda: all_wait(s, j, many * plan_count - 1).wait_send())

    lane = lax.broadcasted_iota(jnp.int32, (cx, cy), 1)
    lane_p = lax.broadcasted_iota(jnp.int32, (cz, cy), 1)

    def new_velocity(s):
        def body(z, unused):
            for c in (1, 3, 5):
                sig[c, z + 1, 7:8, :] = sigp[0, c, pl.ds(z, 1), :]
                sig[c, z + 1, cx + 8 : cx + 9, :] = sigp[1, c, pl.ds(z, 1), :]
            for c in range(3):
                i, j, k = SYM[c]
                force = sig[i, z + 2, own, :] - sig[i, z, own, :]
                force += sig[j, z + 1, pl.ds(9, cx), :] - sig[j, z + 1, pl.ds(7, cx), :]
                force += along_y(sig[k, z + 1, own, :], lane, cy)
                old = v0[c, z] if s == 0 else vx[s - 1, c, z + 2, own, :]
                at = pl.ds(pl.multiple_of(z * cx, 16), cx)
                spot = pl.ds(pl.multiple_of(c * rows + z * cx, 16), cx)
                push = acc_c[spot, :] - count_c[at, :] * old
                new = old + scale[z] * (0.5 * force + push)
                vx[s, c, z + 2, own, :] = new
                if s < STEPS - 1:
                    high, low = split_two(new)
                    thi[spot, :] = high
                    tlo[spot, :] = low
                row = pl.ds(z, 1)
                pbuf[s, 0, c, 0, row, :] = new[0:1]
                pbuf[s, 1, c, 1, row, :] = new[cx - 1 : cx]
                if s < STEPS - 1:
                    pbuf[s, 0, c, 1, row, :] = new[1:2]
                    pbuf[s, 1, c, 0, row, :] = new[cx - 2 : cx - 1]
            return unused

        lax.fori_loop(0, cz, body, 0, unroll=2)
        if s < STEPS - 1:
            for i in range(4):
                z = cz - 1 if i // 2 else 0
                x = cx - 1 if i % 2 else 0
                for c in range(3):
                    cbuf[s, i, c : c + 1, :] = vx[s, c, z + 2, 8 + x : 9 + x, :]

    def halo_leg(s):
        w = 2 if s < STEPS - 1 else 1
        xs0 = pl.ds(0, w)
        xs1 = pl.ds(2 - w, w)
        mid = pl.ds(8, cz)
        send = lambda i: (halo_send.at[s, i], halo_recv.at[s, i])
        copies = []
        if s < STEPS - 1:
            for i in range(4):
                copies.append(remote(cbuf.at[s, i], crx.at[s, i], *send(4 + i), *corners[i]))
        copies += [
            remote(
                vx.at[s, :, pl.ds(cz + 2 - w, w), own, :],
                vx.at[s, :, pl.ds(2 - w, w), own, :],
                *send(0),
                d_up,
                p,
            ),
            remote(
                vx.at[s, :, pl.ds(2, w), own, :],
                vx.at[s, :, pl.ds(cz + 2, w), own, :],
                *send(1),
                d_dn,
                p,
            ),
            remote(pbuf.at[s, 0, :, xs0], rxp.at[s, 1, :, xs0, mid, :], *send(2), d, p_dn),
            remote(pbuf.at[s, 1, :, xs1], rxp.at[s, 0, :, xs1, mid, :], *send(3), d, p_up),
        ]
        return copies

    def new_stress(s):
        last = s == STEPS - 1

        @pl.when(d == 0)
        def _():
            vx[s, :, 0:2, own, :] = jnp.zeros((3, 2, cx, cy), F32)
            if not last:
                crx[s, 2:4] = jnp.zeros((2, 3, cy), F32)

        @pl.when(d == depth_count - 1)
        def _():
            vx[s, :, cz + 2 : cz + 4, own, :] = jnp.zeros((3, 2, cx, cy), F32)
            if not last:
                crx[s, 0:2] = jnp.zeros((2, 3, cy), F32)

        @pl.when(p == 0)
        def _():
            rxp[s, 0, :, :, 8 : 8 + cz, :] = jnp.zeros((3, 2, cz, cy), F32)
            if not last:
                for i in (1, 3):
                    crx[s, i] = jnp.zeros((3, cy), F32)

        @pl.when(p == plan_count - 1)
        def _():
            rxp[s, 1, :, :, 8 : 8 + cz, :] = jnp.zeros((3, 2, cz, cy), F32)
            if not last:
                for i in (0, 2):
                    crx[s, i] = jnp.zeros((3, cy), F32)

        if not last:
            for c in range(3):
                for side in range(2):
                    x = 7 if side == 0 else cx + 8
                    below = crx[s, 3 - side, c : c + 1, :]
                    above = crx[s, 1 - side, c : c + 1, :]
                    vx[s, c, 1, x : x + 1, :] = below
                    vx[s, c, cz + 2, x : x + 1, :] = above
                    rxp[s, side, c, 1 - side, 7:8, :] = below
                    rxp[s, side, c, 1 - side, cz + 8 : cz + 9, :] = above

        def rows_in(z, unused):
            for c in range(3):
                vx[s, c, z + 2, 7:8, :] = rxp[s, 0, c, 1, pl.ds(z + 8, 1), :]
                vx[s, c, z + 2, cx + 8 : cx + 9, :] = rxp[s, 1, c, 0, pl.ds(z + 8, 1), :]
            return unused

        lax.fori_loop(0, cz, rows_in, 0)

        def body(layer, unused):
            dz = [
                vx[s, c, layer + 2, own, :] - vx[s, c, layer, own, :] for c in range(3)
            ]
            dx = [
                vx[s, c, layer + 1, pl.ds(9, cx), :] - vx[s, c, layer + 1, pl.ds(7, cx), :]
                for c in range(3)
            ]
            dy = [along_y(vx[s, c, layer + 1, own, :], lane, cy) for c in range(3)]
            flag = flg[layer]
            new = updated_stress(
                [sig[c, layer, own, :] for c in range(6)], dz, dx, dy, flag == 0, flag == 1
            )
            for c in range(6):
                sig[c, layer, own, :] = new[c]
            return unused

        if last:
            lax.fori_loop(1, cz + 1, body, 0, unroll=2)
            return
        lax.fori_loop(0, cz + 2, body, 0, unroll=2)
        for side in range(2):
            inner = [pbuf[s, side, c, side] for c in range(3)]
            outer = [rxp[s, side, c, side, 8 : 8 + cz, :] for c in range(3)]
            sign = 1.0 if side == 0 else -1.0
            ring = 1 - side
            dz = [
                rxp[s, side, c, ring, 9 : 9 + cz, :] - rxp[s, side, c, ring, 7 : 7 + cz, :]
                for c in range(3)
            ]
            dx = [sign * (inner[c] - outer[c]) for c in range(3)]
            dy = [along_y(rxp[s, side, c, ring, 8 : 8 + cz, :], lane_p, cy) for c in range(3)]
            flag = sigp[side, 6]
            new = updated_stress(
                [sigp[side, c] for c in range(6)], dz, dx, dy, flag == 0.0, flag == 1.0
            )
            for c in range(6):
                sigp[side, c] = new[c]
        clear_outside()

    def clear_outside():
        @pl.when(d == 0)
        def _():
            sig[:, 0, own, :] = jnp.zeros((6, cx, cy), F32)

        @pl.when(d == depth_count - 1)
        def _():
            sig[:, cz + 1, own, :] = jnp.zeros((6, cx, cy), F32)

        @pl.when(p == 0)
        def _():
            sigp[0, 0:6] = jnp.zeros((6, cz, cy), F32)

        @pl.when(p == plan_count - 1)
        def _():
            sigp[1, 0:6] = jnp.zeros((6, cz, cy), F32)

    def start(copies):
        for copy in copies:
            copy.start()
        return copies

    def arrive(copies):
        for copy in copies:
            copy.wait_recv()

    start(init[0:2])
    start_parts(0)
    start(init[2:])
    arrive(init[0:2])
    middle_parts(0)
    start_numbers()
    arrive(init[2:4])
    cell_terms(0)
    arrive(init[4:])
    clear_outside()
    new_velocity(0)
    halos = [start(halo_leg(0))]
    pile_terms(1)
    start_parts(1)
    update_pile(0)
    middle_parts(1)
    own_pile(0)
    arrive(halos[0])
    new_stress(0)
    update_pile(1)
    wait_pile(0)
    cell_terms(1)
    new_velocity(1)
    halos.append(start(halo_leg(1)))
    pile_terms(2)
    start_parts(2)
    own_pile(1)
    middle_parts(2)
    arrive(halos[1])
    new_stress(1)
    wait_pile(1)
    cell_terms(2)
    new_velocity(2)
    halos.append(start(halo_leg(2)))
    velocity_back = pltpu.make_async_copy(
        vx.at[2, :, pl.ds(2, cz), own, :], velocity_out, local_sem.at[0]
    )
    velocity_back.start()
    update_pile(2)
    arrive(halos[2])
    new_stress(2)
    stress_back = pltpu.make_async_copy(
        sig.at[:, pl.ds(1, cz), own, :], stress_out, local_sem.at[1]
    )
    stress_back.start()
    wait_pile(2)

    def pile_lines(t, unused):
        for r in range(8):
            at = pl.ds(pl.multiple_of(t * 1024 + r * 128, 128), 128)
            for c in range(3):
                pilev[c : c + 1, at] = pvw[STEPS, units + c * tiles + t, r : r + 1, :]
        return unused

    lax.fori_loop(0, tiles, pile_lines, 0)
    pile_back = pltpu.make_async_copy(pilev, pile_out, local_sem.at[2])
    pile_back.start()

    for copies in [init] + halos:
        for copy in copies:
            copy.wait_send()
    for s in range(STEPS):
        drain_pile(s)
    velocity_back.wait()
    stress_back.wait()
    pile_back.wait()


def shards(
    depth_count,
    plan_count,
    stress,
    velocity,
    density,
    flags,
    pile_velocity,
    pile_mass,
    jack_force,
    pair_elem,
    pair_cell,
):
    cz, cx, cy = density.shape
    width = pile_mass.shape[0]
    tiles = width // 1024
    pairs = pair_elem.shape[1]
    chunk = min(1024, pairs)
    units = 3 * tiles
    slots = -(-units // plan_count)
    rows = cz * cx
    prows = -(-(3 * width // 256) // 16) * 16
    sizes = (depth_count, plan_count, cz, cx, cy, tiles, pairs, chunk)
    vm = lambda *shape: pltpu.VMEM(shape, F32)
    half = lambda *shape: pltpu.VMEM(shape, BF16)
    whole = lambda *shape: pltpu.VMEM(shape, jnp.int32)
    dma = lambda *shape: pltpu.SemaphoreType.DMA(shape)
    scratch = [
        vm(6, cz + 2, cx + 16, cy),
        vm(STEPS, 3, cz + 4, cx + 16, cy),
        vm(3, cz, cx, cy),
        vm(cz, cx, cy),
        whole(cz + 2, cx, cy),
        vm(2, 7, cz, cy),
        vm(2, 7, cz, cy),
        vm(STEPS, 2, 3, 2, cz, cy),
        vm(STEPS, 2, 3, 2, cz + 16, cy),
        vm(STEPS, 4, 3, cy),
        vm(STEPS, 4, 3, cy),
        vm(STEPS + 1, 3 * units, 8, 128),
        vm(tiles, 8, 128),
        vm(units, 8, 128),
        vm(3, width),
        vm(3, width),
        whole(1, pairs),
        whole(1, pairs),
        whole(1, pairs),
        whole(1, pairs),
        half(cy, pairs),
        half(rows, pairs),
        half(256, pairs),
        half(prows, pairs),
        half(3 * rows, cy),
        half(3 * rows, cy),
        vm(3 * prows, 256),
        half(2, 3 * prows, 256),
        vm(3 * prows, 256),
        vm(3 * rows, cy),
        vm(rows, cy),
        vm(STEPS, 3, units, 8, 128),
        vm(STEPS, 2, units, 8, 128),
        vm(STEPS, units, 8, 128),
        vm(STEPS, slots, 3 * plan_count, 8, 128),
        vm(3, tiles, 8, 128),
        vm(2, tiles, 8, 128),
        vm(tiles, 8, 128),
        vm(slots, plan_count, 8, 128),
        vm(slots, 8, 128),
        dma(9),
        dma(8),
        dma(8),
        dma(STEPS, 8),
        dma(STEPS, 8),
        dma(2),
        dma(2),
        dma(STEPS, slots),
        dma(STEPS, slots),
        dma(slots),
        dma(slots),
        dma(STEPS, slots),
        dma(STEPS, slots),
        dma(STEPS, 2),
        dma(STEPS, 2),
        dma(STEPS, 2),
        dma(STEPS, 2),
    ]
    anywhere = pl.BlockSpec(memory_space=pl.ANY)
    stress, velocity, pile = pl.pallas_call(
        functools.partial(kernel, sizes),
        out_shape=(
            jax.ShapeDtypeStruct(stress.shape, F32),
            jax.ShapeDtypeStruct(velocity.shape, F32),
            jax.ShapeDtypeStruct((3, width), F32),
        ),
        in_specs=[anywhere] * 9,
        out_specs=(anywhere,) * 3,
        scratch_shapes=scratch,
        compiler_params=pltpu.CompilerParams(
            collective_id=0, has_side_effects=True, vmem_limit_bytes=60 * 1024 * 1024
        ),
    )(
        stress,
        velocity,
        density,
        flags,
        pile_velocity,
        pile_mass.reshape(tiles, 8, 128),
        jack_force,
        pair_elem,
        pair_cell,
    )
    return stress, velocity, pile


def solution(mesh):
    field = P(None, "depth", "plan", None)
    cells = P("depth", "plan", None)
    placed = (
        field,
        field,
        cells,
        cells,
        P(None, "depth"),
        P("depth"),
        P(None, "depth"),
        P("depth", "plan"),
        P("depth", "plan"),
    )
    return jax.shard_map(
        functools.partial(shards, mesh.shape["depth"], mesh.shape["plan"]),
        mesh=mesh,
        in_specs=placed,
        out_specs=(field, field, P(None, "depth")),
        check_vma=False,
    )
```
